32 devices in a mesh: block: 4 (over x, core), seq: 2 (over y), mp: 4 (over z).
Axes of the slice: x: 2, y: 2, z: 4, core: 2. Of those that a mesh axis runs over, the one named last changes fastest.
Arguments:
- noisy_latent: float32 [4, 256, 64], P('block', 'seq'), may hold values from -6 to 6
- step_index: int32 [4, 256], P('block', 'seq'), may hold values from 0 to 29
- frame_offset: int32 [4], replicated, may hold values from 0 to 63
- query_input: bfloat16 [4, 256, 2560], P('block', 'seq', 'mp'), may hold values from -6 to 6
- key_input: bfloat16 [4, 256, 2560], P('block', 'seq', 'mp'), may hold values from -6 to 6
- value_input: bfloat16 [4, 256, 2560], P('block', 'seq', 'mp'), may hold values from -6 to 6
- context_keys: bfloat16 [4, 128, 2560], P('block', 'seq', 'mp'), may hold values from -6 to 6
- context_values: bfloat16 [4, 128, 2560], P('block', 'seq', 'mp'), may hold values from -6 to 6
- query_gain: float32 [2560], P('mp'), may hold values from 1 to 2
- key_gain: float32 [2560], P('mp'), may hold values from 1 to 2
- gate_table: float32 [30, 2560], P(None, 'mp'), may hold values from -4 to 4
- head_weight: bfloat16 [2560, 64], P('mp'), may hold values from -0.5 to 0.5
- conv_weight: bfloat16 [3, 3, 3, 16, 384], P(None, None, None, None, 'mp'), may hold values from -0.3125 to 0.3125
- conv_bias: float32 [384], P('mp'), may hold values from -3 to 3
Outputs:
- next_latent: float32 [4, 256, 64], P('block', 'seq')
- decoded: bfloat16 [4, 2, 4, 128, 384], P('block', None, None, 'seq', 'mp')
The draws below stay inside these ranges and needn't reach their ends.
All inputs are finite; a program needn't handle non-finite values.
Results may differ from the reference program's by a relative error of at most 0.0078.
Values may be sent and summed in bfloat16 or wider, within the bound.
A program may use at most 64 MiB of HBM per device.

```python
import math
import jax
import jax.numpy as jnp
import numpy as np
from jax import lax

HEADS = 20
HD = 128
LAT = 16
COUT = 384
STEPS = 30
FRAMES = 2
PW = 64
PCH = 64
PH = 2
CT = 256
CTX = 128
HL = 4
WL = 128
CLIPS = 4


def with_ends(entries, stream_key, smallest, top_value):
    place = [jax.random.randint(jax.random.fold_in(stream_key, axis), (), 0, length) for axis, length in enumerate(entries.shape)]
    longest = entries.shape.index(max(entries.shape))
    beside = place[:longest] + [(place[longest] + 1) % entries.shape[longest]] + place[longest + 1:]
    return entries.at[tuple(place)].set(smallest).at[tuple(beside)].set(top_value)


def steps_of(rng, extent, split, smallest, high):
    gain, own = 1.0, jax.random.fold_in(rng, 6)
    for position, parts in split:
        draws = jnp.exp(jax.random.uniform(jax.random.fold_in(own, position), (parts,), jnp.float32, smallest / len(split), high / len(split)))
        gain = gain * jnp.repeat(draws, extent[position] // parts).reshape([-1 if axis == position else 1 for axis in range(len(extent))])
    return gain


def scatter_about(rng, shape, scale, limit, shards=(), held_as=jnp.bfloat16):
    level = steps_of(rng, shape, shards, -0.22, 0.18) if shards else 1.0
    drawn = jax.random.normal(rng, shape, jnp.float32) * scale * level
    return jnp.minimum(jnp.maximum(drawn, -limit), limit).astype(held_as)


def setup_inputs(seed: int = 0) -> dict:
    key_list = jax.random.split(jax.random.key(seed), 15)
    noisy_latent = scatter_about(key_list[0], (CLIPS, CT, PCH), 1.0, 6.0, ((0, 4), (1, 2)), jnp.float32)
    step_index = with_ends(jax.random.randint(key_list[1], (CLIPS, CT), 0, STEPS), jax.random.fold_in(key_list[1], 1), 0, STEPS - 1).astype(jnp.int32)
    frame_offset = with_ends(jax.random.randint(key_list[2], (CLIPS,), 0, 64), jax.random.fold_in(key_list[2], 1), 0, 63).astype(jnp.int32)
    query_input = scatter_about(key_list[3], (CLIPS, CT, HEADS * HD), 1.0, 6.0, ((0, 4), (1, 2), (2, 4)))
    key_input = scatter_about(key_list[4], (CLIPS, CT, HEADS * HD), 1.0, 6.0, ((0, 4), (1, 2), (2, 4)))
    value_input = scatter_about(key_list[5], (CLIPS, CT, HEADS * HD), 1.0, 6.0, ((0, 4), (1, 2), (2, 4)))
    context_keys = scatter_about(key_list[6], (CLIPS, CTX, HEADS * HD), 1.0, 6.0, ((0, 4), (1, 2), (2, 4)))
    context_values = scatter_about(key_list[7], (CLIPS, CTX, HEADS * HD), 1.0, 6.0, ((0, 4), (1, 2), (2, 4)))
    query_gain = jnp.clip(jnp.exp(math.log(2.0) - 0.6931472 * jax.random.uniform(key_list[8], (HEADS * HD,), jnp.float32) ** steps_of(key_list[8], (HEADS * HD,), ((0, 4),), -0.2, 0.2)), 1.0, 2.0)
    key_gain = jnp.clip(jnp.exp(math.log(2.0) - 0.6931472 * jax.random.uniform(key_list[9], (HEADS * HD,), jnp.float32) ** steps_of(key_list[9], (HEADS * HD,), ((0, 4),), -0.2, 0.2)), 1.0, 2.0)
    gate_table = scatter_about(key_list[10], (STEPS, HEADS * HD), 1.0, 4.0, ((1, 4),), jnp.float32)
    head_weight = scatter_about(key_list[11], (HEADS * HD, PCH), (HEADS * HD // 16) ** -0.5, 0.5, ((0, 4),))
    conv_weight = scatter_about(key_list[12], (3, 3, 3, LAT, COUT), (27 * LAT) ** -0.5, 0.3125, ((4, 4),))
    conv_bias = scatter_about(key_list[13], (COUT,), 0.5, 3.0, ((0, 4),), jnp.float32)
    return dict(noisy_latent=noisy_latent, step_index=step_index, frame_offset=frame_offset, query_input=query_input, key_input=key_input, value_input=value_input, context_keys=context_keys, context_values=context_values, query_gain=query_gain, key_gain=key_gain, gate_table=gate_table, head_weight=head_weight, conv_weight=conv_weight, conv_bias=conv_bias)


shift_factor = 8.0

def frequency_rows():
    pairs_time = (HD - 4 * (HD // 6)) // 2
    pairs_side = HD // 6
    time_part = 10000.0 ** (-np.arange(pairs_time) / pairs_time)
    side_part = 10000.0 ** (-np.arange(pairs_side) / pairs_side)
    blank_time = np.zeros(pairs_time)
    blank_side = np.zeros(pairs_side)
    along_time = np.concatenate([time_part, blank_side, blank_side])
    along_rows = np.concatenate([blank_time, side_part, blank_side])
    along_cols = np.concatenate([blank_time, blank_side, side_part])
    return (jnp.asarray(along_time, jnp.float32), jnp.asarray(along_rows, jnp.float32), jnp.asarray(along_cols, jnp.float32))

def normalize_rotate(raw_input, gain_row, time_pos, row_pos, col_pos):
    amount = raw_input.shape[0]
    head_count = raw_input.shape[1] // HD
    values = raw_input.astype(jnp.float32).reshape(amount, head_count, HD)
    factor = lax.rsqrt(lax.optimization_barrier(jnp.mean(values * values, axis=(1, 2), keepdims=True)) + 1e-06)
    values = values * factor * gain_row.astype(jnp.float32).reshape(1, head_count, HD)
    along_time, along_rows, along_cols = frequency_rows()
    angles = time_pos[:, None] * along_time[None, :] + row_pos[:, None] * along_rows[None, :] + col_pos[:, None] * along_cols[None, :]
    cosine = jnp.cos(angles)[:, None, :]
    sine_part = jnp.sin(angles)[:, None, :]
    paired = values.reshape(amount, head_count, HD // 2, 2)
    real_part = paired[..., 0]
    imag_part = paired[..., 1]
    turned = jnp.stack([real_part * cosine - imag_part * sine_part, real_part * sine_part + imag_part * cosine], axis=-1)
    return turned.reshape(amount, head_count * HD).astype(jnp.bfloat16)

def noise_level(level_now):
    remain = 1.0 - level_now / STEPS
    return shift_factor * remain / (1.0 + (shift_factor - 1.0) * remain)

def lift_tokens(tokens, columns, grid_rows):
    shaped = tokens.reshape(FRAMES, grid_rows, columns, 2, 2, LAT)
    return shaped.transpose(0, 1, 3, 2, 4, 5).reshape(FRAMES, 2 * grid_rows, 2 * columns, LAT)

def convolve(padded, conv_weight, conv_bias):
    frames_out = padded.shape[0] - 2
    height = padded.shape[1] - 2
    span_cols = padded.shape[2] - 2
    pieces = []
    for time_tap in range(3):
        for row_tap in range(3):
            for col_tap in range(3):
                pieces.append(padded[time_tap:time_tap + frames_out, row_tap:row_tap + height, col_tap:col_tap + span_cols, :])
    stacked = jnp.stack(pieces, axis=3).reshape(frames_out * height * span_cols, 27 * LAT)
    flat_weight = conv_weight.reshape(27 * LAT, conv_weight.shape[-1])
    summed = jnp.einsum('rk,ko->ro', stacked.astype(jnp.float32), flat_weight.astype(jnp.float32))
    summed = summed + conv_bias.astype(jnp.float32)[None, :]
    return summed.astype(jnp.bfloat16).reshape(frames_out, height, span_cols, -1)

def attend_all(queries, all_keys, all_values, inverse_root):
    head_query = queries.reshape(-1, HEADS, HD).transpose(1, 0, 2)
    head_key = all_keys.reshape(-1, HEADS, HD).transpose(1, 0, 2)
    head_value = all_values.reshape(-1, HEADS, HD).transpose(1, 0, 2)

    def per_head(triple):
        query_head, key_head, value_head = triple
        scores = jnp.einsum('qd,kd->qk', query_head.astype(jnp.float32), key_head.astype(jnp.float32)) * inverse_root
        expon = jnp.exp(scores)
        rounded = lax.optimization_barrier(expon.astype(jnp.bfloat16)).astype(jnp.float32)
        numer = jnp.einsum('qk,kd->qd', rounded, value_head.astype(jnp.float32))
        return numer / lax.optimization_barrier(jnp.sum(expon, axis=1, keepdims=True))
    result = lax.map(per_head, (head_query, head_key, head_value))
    return result.transpose(1, 0, 2).reshape(-1, HEADS * HD)

def reference(noisy_latent, step_index, frame_offset, query_input, key_input, value_input, context_keys, context_values, query_gain, key_gain, gate_table, head_weight, conv_weight, conv_bias):
    inverse_root = 1.0 / math.sqrt(HD)
    token_ids = jnp.arange(CT, dtype=jnp.int32)
    frame_ids = token_ids // (PH * PW)
    row_ids = (token_ids // PW % PH).astype(jnp.float32)
    col_ids = (token_ids % PW).astype(jnp.float32)
    context_ids = jnp.arange(CTX, dtype=jnp.int32)
    context_rows = (context_ids // PW).astype(jnp.float32)
    context_cols = (context_ids % PW).astype(jnp.float32)
    earlier = jnp.zeros((2, HL, WL, LAT), jnp.bfloat16)
    next_list = []
    decoded_list = []
    for clip_index in range(CLIPS):
        moment = (frame_offset[clip_index] + frame_ids).astype(jnp.float32)
        queries = normalize_rotate(query_input[clip_index], query_gain, moment, row_ids, col_ids)
        own_keys = normalize_rotate(key_input[clip_index], key_gain, moment, row_ids, col_ids)
        all_keys = own_keys
        all_values = value_input[clip_index]
        if clip_index > 0:
            context_moment = jnp.zeros((CTX,), jnp.float32) + (frame_offset[clip_index - 1] + FRAMES - 1).astype(jnp.float32)
            prior_keys = normalize_rotate(context_keys[clip_index - 1], key_gain, context_moment, context_rows, context_cols)
            all_keys = jnp.concatenate([own_keys, prior_keys], 0)
            all_values = jnp.concatenate([value_input[clip_index], context_values[clip_index - 1]], 0)
        attention = attend_all(queries, all_keys, all_values, inverse_root)
        gate_rows = gate_table[step_index[clip_index]]
        gated_out = (attention * gate_rows).astype(jnp.bfloat16)
        velocity = jnp.dot(gated_out, head_weight, preferred_element_type=jnp.float32)
        level_now = step_index[clip_index].astype(jnp.float32)
        now_sigma = noise_level(level_now)[:, None]
        next_sigma = noise_level(level_now + 1.0)[:, None]
        latent_now = noisy_latent[clip_index]
        next_list.append(latent_now + (next_sigma - now_sigma) * velocity)
        clean_tokens = (latent_now - now_sigma * velocity).astype(jnp.bfloat16)
        latent = lift_tokens(clean_tokens.reshape(FRAMES * PH, PW, 4 * LAT), PW, PH)
        framed = jnp.concatenate([earlier, latent], 0)
        padded = jnp.pad(framed, ((0, 0), (1, 1), (1, 1), (0, 0)))
        decoded_list.append(convolve(padded, conv_weight, conv_bias))
        earlier = latent[FRAMES - 2:]
    return (jnp.stack(next_list), jnp.stack(decoded_list))
```

```python
import math

import jax
import jax.numpy as jnp
import numpy as np
from jax import lax
from jax.experimental import pallas as pl
from jax.experimental.pallas import tpu as pltpu
from jax.sharding import PartitionSpec as P

HEADS = 20
HD = 128
LAT = 16
STEPS = 30
FRAMES = 2
PW = 64
RDEV = 2


shift_factor = 8.0


def passed_along(x, axis, by):
    devices = lax.axis_size(axis)
    pairs = [(i, i + by) for i in range(devices) if 0 <= i + by < devices]
    return lax.ppermute(x, axis, pairs)


def padded_2(x, sides, width):
    for axis, dim in sides:
        devices, length = (lax.axis_size(axis), x.shape[dim])
        up = [(i, (i + 1) % devices) for i in range(devices - 1)]
        down = [(j, i) for i, j in up]
        last = lax.slice_in_dim(x, length - width, length, axis=dim)
        initial = lax.slice_in_dim(x, 0, width, axis=dim)
        before = lax.ppermute(last, axis, up)
        after = lax.ppermute(initial, axis, down)
        x = jnp.concatenate([before, x, after], axis=dim)
    return x


def frequency_rows():
    pairs_time = (HD - 4 * (HD // 6)) // 2
    pairs_side = HD // 6
    time_part = 10000.0 ** (-np.arange(pairs_time) / pairs_time)
    side_part = 10000.0 ** (-np.arange(pairs_side) / pairs_side)
    blank_time = np.zeros(pairs_time)
    blank_side = np.zeros(pairs_side)
    along_time = np.concatenate([time_part, blank_side, blank_side])
    along_rows = np.concatenate([blank_time, side_part, blank_side])
    along_cols = np.concatenate([blank_time, blank_side, side_part])
    return (
        jnp.asarray(along_time, jnp.float32),
        jnp.asarray(along_rows, jnp.float32),
        jnp.asarray(along_cols, jnp.float32),
    )


def square_total(raw_input):
    values = raw_input.astype(jnp.float32)
    return jnp.sum(values * values, axis=1)


def normalize_rotate(raw_input, total_sq, gain_row, time_pos, row_pos, col_pos):
    amount = raw_input.shape[0]
    head_count = raw_input.shape[1] // HD
    values = raw_input.astype(jnp.float32).reshape(amount, head_count, HD)
    factor = lax.rsqrt(total_sq / (HEADS * HD) + 1e-06)[:, None, None]
    values = values * factor * gain_row.reshape(1, head_count, HD)
    along_time, along_rows, along_cols = frequency_rows()
    angles = (
        time_pos[:, None] * along_time[None, :]
        + row_pos[:, None] * along_rows[None, :]
        + col_pos[:, None] * along_cols[None, :]
    )
    cosine = jnp.cos(angles)[:, None, :]
    sine_part = jnp.sin(angles)[:, None, :]
    paired = values.reshape(amount, head_count, HD // 2, 2)
    real_part = paired[..., 0]
    imag_part = paired[..., 1]
    turned = jnp.stack(
        [real_part * cosine - imag_part * sine_part, real_part * sine_part + imag_part * cosine],
        axis=-1,
    )
    return turned.reshape(amount, head_count * HD).astype(jnp.bfloat16)


def noise_level(level_now):
    remain = 1.0 - level_now / STEPS
    return shift_factor * remain / (1.0 + (shift_factor - 1.0) * remain)


def lift_tokens(tokens, columns, grid_rows):
    shaped = tokens.reshape(FRAMES, grid_rows, columns, 2, 2, LAT)
    return shaped.transpose(0, 1, 3, 2, 4, 5).reshape(FRAMES, 2 * grid_rows, 2 * columns, LAT)


def convolve(padded, conv_weight, conv_bias):
    frames_out = padded.shape[0] - 2
    height = padded.shape[1] - 2
    span_cols = padded.shape[2] - 2
    pieces = []
    for time_tap in range(3):
        for row_tap in range(3):
            for col_tap in range(3):
                pieces.append(
                    padded[
                        time_tap : time_tap + frames_out,
                        row_tap : row_tap + height,
                        col_tap : col_tap + span_cols,
                        :,
                    ]
                )
    stacked = jnp.stack(pieces, axis=3).reshape(frames_out * height * span_cols, 27 * LAT)
    flat_weight = conv_weight.reshape(27 * LAT, conv_weight.shape[-1])
    summed = jnp.dot(stacked, flat_weight, preferred_element_type=jnp.float32)
    summed = summed + conv_bias[None, :]
    return summed.astype(jnp.bfloat16).reshape(frames_out, height, span_cols, -1)


def with_cache(slab):
    earlier = passed_along(slab, "block", 1)
    return jnp.concatenate([earlier, slab], 0)


def body(
    noisy_latent,
    step_index,
    frame_offset,
    query_input,
    key_input,
    value_input,
    context_keys,
    context_values,
    query_gain,
    key_gain,
    gate_table,
    head_weight,
    conv_weight,
    conv_bias,
):
    clip_pos = lax.axis_index("block")
    seq_pos = lax.axis_index("seq")
    seq_count = lax.axis_size("seq")
    tok_rows = query_input.shape[1]
    ctx_rows = context_keys.shape[1]
    local_width = query_input.shape[2]
    local_heads = local_width // HD
    grid_rows = RDEV * seq_count // FRAMES
    inverse_root = 1.0 / math.sqrt(HD)
    relayed = passed_along(jnp.stack([context_keys[0], context_values[0]]), "block", 1)
    query_sq, key_sq, prior_sq = lax.psum(
        (square_total(query_input[0]), square_total(key_input[0]), square_total(relayed[0])), "mp"
    )
    token_ids = seq_pos * tok_rows + jnp.arange(tok_rows, dtype=jnp.int32)
    frame_ids = token_ids // (grid_rows * PW)
    row_ids = (token_ids // PW % grid_rows).astype(jnp.float32)
    col_ids = (token_ids % PW).astype(jnp.float32)
    own_offset = lax.dynamic_index_in_dim(frame_offset, clip_pos, 0, keepdims=False)
    prior_offset = lax.dynamic_index_in_dim(
        frame_offset, jnp.maximum(clip_pos - 1, 0), 0, keepdims=False
    )
    moment = (own_offset + frame_ids).astype(jnp.float32)
    queries = normalize_rotate(query_input[0], query_sq, query_gain, moment, row_ids, col_ids)
    own_keys = normalize_rotate(key_input[0], key_sq, key_gain, moment, row_ids, col_ids)
    own_values = value_input[0]
    context_ids = seq_pos * ctx_rows + jnp.arange(ctx_rows, dtype=jnp.int32)
    context_moment = jnp.zeros((ctx_rows,), jnp.float32) + (prior_offset + FRAMES - 1).astype(
        jnp.float32
    )
    prior_rot = normalize_rotate(
        relayed[0],
        prior_sq,
        key_gain,
        context_moment,
        (context_ids // PW).astype(jnp.float32),
        (context_ids % PW).astype(jnp.float32),
    )
    prior_values = relayed[1]
    keep_prior = (clip_pos > 0).astype(jnp.float32)
    start_state = (
        jnp.zeros((tok_rows, local_width), jnp.float32),
        jnp.zeros((tok_rows, local_heads), jnp.float32),
    )
    joint_rows = tok_rows + ctx_rows
    joint_keys = jnp.concatenate([own_keys, prior_rot], 0)
    joint_values = jnp.concatenate([own_values, prior_values], 0)
    piece = (
        lax.all_gather(joint_keys, "seq", axis=0, tiled=True),
        lax.all_gather(joint_values, "seq", axis=0, tiled=True),
    )
    local_rows = jnp.arange(piece[0].shape[0], dtype=jnp.int32) % joint_rows
    row_keep = jnp.where(local_rows < tok_rows, 1.0, keep_prior)
    key_piece = piece[0]
    value_piece = piece[1]

    def per_head(head_slot, state):
        numer, denom = state
        query_head = lax.dynamic_slice_in_dim(queries, head_slot * HD, HD, 1)
        key_head = lax.dynamic_slice_in_dim(key_piece, head_slot * HD, HD, 1)
        value_head = lax.dynamic_slice_in_dim(value_piece, head_slot * HD, HD, 1)
        scores = (
            jnp.einsum("qd,kd->qk", query_head, key_head, preferred_element_type=jnp.float32)
            * inverse_root
        )
        expon = jnp.exp(scores) * row_keep[None, :]
        added = jnp.dot(expon.astype(jnp.bfloat16), value_head, preferred_element_type=jnp.float32)
        old_numer = lax.dynamic_slice_in_dim(numer, head_slot * HD, HD, 1)
        numer = lax.dynamic_update_slice_in_dim(numer, old_numer + added, head_slot * HD, 1)
        old_denom = lax.dynamic_slice_in_dim(denom, head_slot, 1, 1)
        denom = lax.dynamic_update_slice_in_dim(
            denom, old_denom + jnp.sum(expon, axis=1, keepdims=True), head_slot, 1
        )
        return (numer, denom)

    state = lax.fori_loop(0, local_heads, per_head, start_state)
    numer, denom = state
    attention = (numer.reshape(tok_rows, local_heads, HD) / denom[:, :, None]).reshape(
        tok_rows, local_width
    )
    one_hot = (step_index[0][:, None] == jnp.arange(STEPS, dtype=jnp.int32)[None, :]).astype(
        jnp.float32
    )
    gate_rows = jnp.dot(one_hot, gate_table, precision=lax.Precision.HIGHEST)
    gated_out = (attention * gate_rows).astype(jnp.bfloat16)
    partial_sum = jnp.dot(gated_out, head_weight, preferred_element_type=jnp.float32)
    velocity = lax.psum(partial_sum, "mp")
    level_now = step_index[0].astype(jnp.float32)
    now_sigma = noise_level(level_now)[:, None]
    next_sigma = noise_level(level_now + 1.0)[:, None]
    latent_now = noisy_latent[0]
    next_latent = latent_now + (next_sigma - now_sigma) * velocity
    clean_tokens = (latent_now - now_sigma * velocity).astype(jnp.bfloat16)
    slab_cols = PW // seq_count
    rows_local = clean_tokens.reshape(RDEV, PW, clean_tokens.shape[1])
    moved = lax.all_to_all(rows_local, "seq", split_axis=1, concat_axis=0, tiled=True)
    slab = lift_tokens(moved, slab_cols, grid_rows)
    framed = padded_2(with_cache(slab), (("seq", 2),), 1)
    framed = jnp.pad(framed, ((0, 0), (1, 1), (0, 0), (0, 0)))
    decoded = convolve(framed, conv_weight, conv_bias)
    return (next_latent[None], decoded[None])


def wave_rows():
    pairs_side = HD // 6
    pairs_time = (HD - 4 * pairs_side) // 2
    table = np.zeros((8, HD), np.float32)
    for lane in range(HD):
        pair = lane // 2
        if pair < pairs_time:
            table[0, lane] = np.float32(10000.0 ** (-pair / pairs_time))
        elif pair < pairs_time + pairs_side:
            table[1, lane] = np.float32(10000.0 ** (-(pair - pairs_time) / pairs_side))
        else:
            table[2, lane] = np.float32(10000.0 ** (-(pair - pairs_time - pairs_side) / pairs_side))
            table[3, lane] = 1.0
    return table


MESH = pl.DeviceIdType.MESH
F32 = jnp.float32
BF16 = jnp.bfloat16
NB, NS, NM = 4, 2, 4
TOK, CTXR, WID, NH = 128, 64, 640, 5
KEYS = TOK + CTXR


def dot(a, b):
    return lax.dot_general(a, b, (((1,), (0,)), ((), ())), preferred_element_type=F32)


def dot_nt(a, b):
    return lax.dot_general(a, b, (((1,), (1,)), ((), ())), preferred_element_type=F32)


def dot_tn(a, b):
    return lax.dot_general(a, b, (((0,), (0,)), ((), ())), preferred_element_type=F32)


def step_kernel(
    fo, noisy, step, q_in, k_in, v_in, ck_in, cv_in, qg, kg, gate, hw, cw, cb, waves,
    next_out, dec_out,
    qall, kbuf, vctx, ckrot, vt, wt, ebuf, numer, st_own, st_prev, dmine, dother, gatet,
    part, rs, nl, lp, nz, sig_now, sig_step, wbig, fr, stage,
    q_send, q_recv, c_send, c_recv, s_send, s_recv, sp_recv, d_send, d_recv,
    r_send, r_recv, n_send, n_recv, l_send, l_recv,
):
    b = lax.axis_index("block")
    s = lax.axis_index("seq")
    m = lax.axis_index("mp")
    nb = lax.rem(b + 1, NB)
    pb = lax.rem(b + NB - 1, NB)
    other = 1 - s

    barrier = pltpu.get_barrier_semaphore()
    for ds in range(NS):
        for dm in range(NM):
            ss, mm = lax.rem(s + ds, NS), lax.rem(m + dm, NM)
            if ds or dm:
                pl.semaphore_signal(barrier, inc=1, device_id=(b, ss, mm), device_id_type=MESH)
            pl.semaphore_signal(barrier, inc=1, device_id=(pb, ss, mm), device_id_type=MESH)

    lane = lax.broadcasted_iota(jnp.int32, (8, HD), 1)
    even = lax.rem(lane, 2) == 0
    sign = jnp.where(even, -1.0, 1.0)[0:1]
    row8 = lax.broadcasted_iota(jnp.int32, (8, HD), 0)
    base = fo[b]
    tau = jnp.where(row8 == 2, base + 1, base + s).astype(F32)
    hpos = jnp.where(row8 == 2, s, jnp.where(row8 == 1, 1, 0)).astype(F32)
    ang = tau * waves[0:1] + hpos * waves[1:2]
    cos_r, sin_r = jnp.cos(ang), jnp.sin(ang)
    wpos = lax.broadcasted_iota(jnp.int32, (64, HD), 0).astype(F32)
    ang_c = wpos * waves[2:3]
    cos_c, sin_c = jnp.cos(ang_c), jnp.sin(ang_c)
    col_lane = jnp.broadcast_to(waves[3:4], (64, HD)) > 0.5

    def table(r):
        c = jnp.where(col_lane, cos_c, jnp.broadcast_to(cos_r[r : r + 1], (64, HD)))
        n = jnp.where(col_lane, sin_c, jnp.broadcast_to(sin_r[r : r + 1], (64, HD)))
        return c, n * sign

    c0, n0 = table(0)
    c1, n1 = table(1)
    cos_t = jnp.concatenate([c0, c1], 0)
    sin_t = jnp.concatenate([n0, n1], 0)
    cos_x, sin_x = table(2)

    pr = lax.broadcasted_iota(jnp.int32, (HD, HD), 0)
    pc = lax.broadcasted_iota(jnp.int32, (HD, HD), 1)
    swap = jnp.where(pc == pr + 1 - 2 * lax.rem(pr, 2), 1.0, 0.0).astype(BF16)

    def swapped(g):
        g8 = jnp.broadcast_to(g, (8, HD))
        return jnp.where(even, pltpu.roll(g8, HD - 1, 1), pltpu.roll(g8, 1, 1))[0:1]

    def rotated(x_ref, gain, ct, st, store):
        total = None
        for h in range(NH):
            sl = slice(h * HD, (h + 1) * HD)
            xb = x_ref[0, :, sl]
            x = xb.astype(F32)
            g = gain[:, sl]
            xs = dot(xb, swap)
            store(sl, ((x * g) * ct + (xs * swapped(g)) * st).astype(BF16))
            total = x * x if total is None else total + x * x
        return total

    def store_q(sl, val):
        qall[s, :, sl] = val

    def store_k(sl, val):
        kbuf[0:TOK, sl] = val

    def store_c(sl, val):
        ckrot[:, sl] = val

    sq_q = rotated(q_in, qg, cos_t, sin_t, store_q)
    sq_c = rotated(ck_in, kg, cos_x, sin_x, store_c)
    sq_k = rotated(k_in, kg, cos_t, sin_t, store_k)
    row_q = jnp.sum(sq_q.T, axis=0, keepdims=True)
    row_k = jnp.sum(sq_k.T, axis=0, keepdims=True)
    sq_c2 = jnp.concatenate([sq_c, jnp.zeros((64, HD), F32)], 0)
    row_c = jnp.sum(sq_c2.T, axis=0, keepdims=True)
    step_row = step[...].astype(F32)
    st_own[s, m] = jnp.where(
        row8 == 0, row_q, jnp.where(row8 == 1, row_k, jnp.where(row8 == 2, row_c, step_row))
    )

    pl.semaphore_wait(barrier, 2 * NS * NM - 1)

    def remote(src, dst, send, recv, dev):
        return pltpu.make_async_remote_copy(
            src_ref=src, dst_ref=dst, send_sem=send, recv_sem=recv, device_id=dev,
            device_id_type=MESH,
        )

    pend = []

    def go(*args):
        copy = remote(*args)
        copy.start()
        pend.append(copy)

    go(qall.at[s], qall.at[s], q_send, q_recv, (b, other, m))
    go(ckrot, kbuf.at[pl.ds(TOK, CTXR)], c_send.at[0], c_recv.at[0], (nb, s, m))
    go(cv_in.at[0], vctx, c_send.at[1], c_recv.at[1], (nb, s, m))
    i = 0
    for ds in range(NS):
        for dm in range(NM):
            ss, mm = lax.rem(s + ds, NS), lax.rem(m + dm, NM)
            if ds or dm:
                go(st_own.at[s, m], st_own.at[s, m], s_send.at[i], s_recv.at[s, m], (b, ss, mm))
                i += 1
    for dm in range(NM):
        mm = lax.rem(m + dm, NM)
        go(st_own.at[s, m], st_prev.at[m], s_send.at[i], sp_recv.at[m], (nb, s, mm))
        i += 1

    for h in range(NH):
        sl = slice(h * HD, (h + 1) * HD)
        vt[sl, 0:TOK] = v_in[0, :, sl].astype(F32).T.astype(BF16)
        wt[:, sl] = hw[sl, :].astype(F32).T.astype(BF16)
    steps_col = jnp.broadcast_to(step_row, (HD, HD)).T
    lane64 = lax.broadcasted_iota(jnp.int32, (64, HD), 1)
    steps2 = jnp.where(lane64 < 64, steps_col[0:64], steps_col[64:128])
    nz[...] = jnp.concatenate([noisy[0, 0:64], noisy[0, 64:128]], 1)

    def level(at):
        remain = 1.0 - at / STEPS
        return 8.0 * remain / (1.0 + 7.0 * remain)

    now = level(steps2)
    sig_now[...] = now
    sig_step[...] = level(steps2 + 1.0) - now
    lp[:, :, 0:16, :] = jnp.zeros((2, 2, 16, HD), BF16)
    lp[:, :, 80:96, :] = jnp.zeros((2, 2, 16, HD), BF16)
    wbig[...] = jnp.zeros(wbig.shape, BF16)
    for qo in range(2):
        for a in range(3):
            for j in range(2):
                for qi in range(2):
                    d = qo + 2 * j + qi - 1
                    if not 0 <= d <= 2:
                        continue
                    for y in range(4):
                        for yo in range(4):
                            t = y - yo + 1
                            if not 0 <= t <= 2:
                                continue
                            r = a * 256 + j * 128 + y * 32 + qi * 16
                            wbig[qo, r : r + 16, yo * 128 : yo * 128 + 96] = cw[a, t, d]

    for ds in range(NS):
        for dm in range(NM):
            if ds or dm:
                ss, mm = lax.rem(s + ds, NS), lax.rem(m + dm, NM)
                remote(st_own.at[ss, mm], st_own.at[ss, mm], s_send.at[0], s_recv.at[ss, mm],
                       (b, other, m)).wait_recv()
    for mm in range(NM):
        remote(st_prev.at[mm], st_prev.at[mm], s_send.at[0], sp_recv.at[mm],
               (b, other, m)).wait_recv()
    inv = 1.0 / (HEADS * HD)
    qstat = [st_own[e, 0] + st_own[e, 1] + st_own[e, 2] + st_own[e, 3] for e in range(NS)]
    kstat = st_own[s, 0] + st_own[s, 1] + st_own[s, 2] + st_own[s, 3]
    cstat = st_prev[0] + st_prev[1] + st_prev[2] + st_prev[3]
    scale = 1.4426950408889634 / math.sqrt(HD)
    fq = [lax.rsqrt(x[0:1] * inv + 1e-06) * scale for x in qstat]
    fk_own = jnp.broadcast_to(lax.rsqrt(kstat[1:2] * inv + 1e-06), (HD, HD)).T
    fk_ctx = jnp.broadcast_to(lax.rsqrt(cstat[2:3] * inv + 1e-06), (HD, HD)).T[0:CTXR]
    fk = jnp.concatenate([fk_own, fk_ctx], 0)
    factor = jnp.concatenate([fk * fq[0], fk * fq[1]], 1)

    steps_all = jnp.concatenate([st_own[0, 0][3:4], st_own[1, 0][3:4]], 1)
    which = lax.broadcasted_iota(jnp.int32, (STEPS, 2 * TOK), 0).astype(F32)
    hot = jnp.where(which == steps_all, 1.0, 0.0).astype(BF16)
    g_all = gate[...]
    g_hi = g_all.astype(BF16)
    g_lo = (g_all - g_hi.astype(F32)).astype(BF16)
    gatet[...] = dot_tn(g_hi, hot) + dot_tn(g_lo, hot)

    remote(ckrot, kbuf.at[pl.ds(TOK, CTXR)], c_send.at[0], c_recv.at[0], (b, other, m)).wait_recv()
    remote(vctx, vctx, c_send.at[1], c_recv.at[1], (b, other, m)).wait_recv()
    for h in range(NH):
        sl = slice(h * HD, (h + 1) * HD)
        vt[sl, TOK:KEYS] = vctx[:, sl].astype(F32).T.astype(BF16)
    remote(qall.at[other], qall.at[other], q_send, q_recv, (b, other, m)).wait_recv()

    has_prior = jnp.broadcast_to(b, (CTXR, 2 * TOK)) > 0
    sub = lax.broadcasted_iota(jnp.int32, (8, 2 * TOK), 0)
    sums = jnp.ones((8, 2 * TOK), F32)
    for h in range(NH):
        sl = slice(h * HD, (h + 1) * HD)
        qh = jnp.concatenate([qall[0, :, sl], qall[1, :, sl]], 0)
        sc = dot_nt(kbuf[:, sl], qh) * factor
        e = jnp.exp2(sc)
        e_own = e[0:TOK]
        e_ctx = jnp.where(has_prior, e[TOK:KEYS], 0.0)
        den = jnp.sum(e_own, axis=0, keepdims=True) + jnp.sum(e_ctx, axis=0, keepdims=True)
        sums = jnp.where(sub == h, den, sums)
        ebuf[h, 0:TOK] = e_own.astype(BF16)
        ebuf[h, TOK:KEYS] = e_ctx.astype(BF16)
    dmine[...] = sums
    go(dmine, dother, d_send, d_recv, (b, other, m))
    for h in range(NH):
        sl = slice(h * HD, (h + 1) * HD)
        numer[sl] = dot(vt[sl, :], ebuf[h]) * gatet[sl]
    remote(dmine, dother, d_send, d_recv, (b, other, m)).wait_recv()
    recip = 1.0 / (dmine[...] + dother[...])
    vel_t = jnp.zeros((64, 2 * TOK), F32)
    for h in range(NH):
        sl = slice(h * HD, (h + 1) * HD)
        vel_t += dot(wt[:, sl], (numer[sl] * recip[h : h + 1]).astype(BF16))
    for f in range(2):
        t = jnp.concatenate([vel_t[:, f * TOK : (f + 1) * TOK], jnp.zeros((64, HD), F32)], 0).T
        part[f] = jnp.concatenate([t[0:64, 0:64], t[64:128, 0:64]], 1)

    def cols(mm):
        return pl.ds(pl.multiple_of(mm * 16, 16), 16)

    def lcols(mm):
        return pl.ds(pl.multiple_of(mm * 16 + 16, 16), 16)

    i = 0
    for ds in range(NS):
        for dm in range(NM):
            if ds or dm:
                ss, mm = lax.rem(s + ds, NS), lax.rem(m + dm, NM)
                go(part.at[ss, cols(mm)], rs.at[s, m], r_send.at[i], r_recv.at[s, m], (b, ss, mm))
                i += 1
    rs[s, m] = part[s, cols(m)]
    for ds in range(NS):
        for dm in range(NM):
            if ds or dm:
                ss, mm = lax.rem(s + ds, NS), lax.rem(m + dm, NM)
                remote(rs.at[ss, mm], rs.at[ss, mm], r_send.at[0], r_recv.at[ss, mm],
                       (b, other, m)).wait_recv()
    vel = rs[0, 0]
    for e in range(1, NS * NM):
        vel = vel + rs[e // NM, e % NM]
    latent = nz[cols(m), :]
    lp[1, s, lcols(m), :] = (latent - sig_now[cols(m), :] * vel).astype(BF16)
    mine = lp.at[1, s, lcols(m)]
    i = 0
    for ds in range(NS):
        for dm in range(NM):
            ss, mm = lax.rem(s + ds, NS), lax.rem(m + dm, NM)
            go(mine, lp.at[0, s, lcols(m)], l_send.at[i], l_recv.at[0, s, m], (nb, ss, mm))
            i += 1
            if ds or dm:
                go(mine, mine, l_send.at[i], l_recv.at[1, s, m], (b, ss, mm))
                i += 1
    nl[cols(m), :] = latent + sig_step[cols(m), :] * vel
    for dm in range(1, NM):
        mm = lax.rem(m + dm, NM)
        go(nl.at[cols(m)], nl.at[cols(m)], n_send.at[dm - 1], n_recv.at[m], (b, s, mm))

    for c in (1, 0):
        for ds in range(NS):
            for dm in range(NM):
                if c == 0 or ds or dm:
                    ss, mm = lax.rem(s + ds, NS), lax.rem(m + dm, NM)
                    at = lp.at[c, ss, lcols(mm)]
                    remote(at, at, l_send.at[0], l_recv.at[c, ss, mm], (b, other, m)).wait_recv()
    slab = pl.ds(pl.multiple_of(s * 32, 32), 64)
    prior2 = jnp.broadcast_to(b, (64, HD)) > 0
    for f in range(2):
        fr[f] = jnp.where(prior2, lp[0, f, slab, :].astype(F32), 0.0)
        fr[2 + f] = lp[1, f, slab, :].astype(F32)
    bias = cb[...]
    for qo in range(2):
        rows = []
        for t in range(2):
            taps = []
            for a in range(3):
                for j in range(2):
                    taps.append(fr[t + a, 15 + qo + j : 47 + qo + j, :].astype(BF16))
            rows.append(jnp.concatenate(taps, 1))
        res = dot(jnp.concatenate(rows, 0), wbig[qo])
        for t in range(2):
            for y in range(4):
                stage[t * 4 + y, pl.ds(qo, 32, stride=2), :] = res[
                    t * 32 : (t + 1) * 32, y * 128 : (y + 1) * 128
                ]
    for t in range(2):
        for y in range(4):
            dec_out[0, t, y] = (stage[t * 4 + y][:, 0:96] + bias).astype(BF16)

    for dm in range(1, NM):
        mm = lax.rem(m + dm, NM)
        remote(nl.at[cols(mm)], nl.at[cols(mm)], n_send.at[0], n_recv.at[mm],
               (b, other, m)).wait_recv()
    final = nl[...]
    next_out[0, 0:64] = final[:, 0:64]
    next_out[0, 64:128] = final[:, 64:128]
    for copy in pend:
        copy.wait_send()


def fused_body(
    noisy_latent, step_index, frame_offset, query_input, key_input, value_input, context_keys,
    context_values, query_gain, key_gain, gate_table, head_weight, conv_weight, conv_bias,
):
    vmem = pl.BlockSpec(memory_space=pltpu.VMEM)
    dma = pltpu.SemaphoreType.DMA
    scratch = [
        pltpu.VMEM((2, TOK, WID), BF16),
        pltpu.VMEM((KEYS, WID), BF16),
        pltpu.VMEM((CTXR, WID), BF16),
        pltpu.VMEM((CTXR, WID), BF16),
        pltpu.VMEM((WID, KEYS), BF16),
        pltpu.VMEM((64, WID), BF16),
        pltpu.VMEM((NH, KEYS, 2 * TOK), BF16),
        pltpu.VMEM((WID, 2 * TOK), F32),
        pltpu.VMEM((NS, NM, 8, HD), F32),
        pltpu.VMEM((NM, 8, HD), F32),
        pltpu.VMEM((8, 2 * TOK), F32),
        pltpu.VMEM((8, 2 * TOK), F32),
        pltpu.VMEM((WID, 2 * TOK), F32),
        pltpu.VMEM((2, 64, HD), F32),
        pltpu.VMEM((NS, NM, 16, HD), F32),
        pltpu.VMEM((64, HD), F32),
        pltpu.VMEM((2, 2, 96, HD), BF16),
        pltpu.VMEM((64, HD), F32),
        pltpu.VMEM((64, HD), F32),
        pltpu.VMEM((64, HD), F32),
        pltpu.VMEM((2, 768, 512), BF16),
        pltpu.VMEM((4, 64, HD), F32),
        pltpu.VMEM((8, 64, HD), F32),
        dma, dma, dma((2,)), dma((2,)),
        dma((11,)), dma((NS, NM)), dma((NM,)),
        dma, dma,
        dma((7,)), dma((NS, NM)),
        dma((3,)), dma((NM,)),
        dma((15,)), dma((2, NS, NM)),
    ]
    return pl.pallas_call(
        step_kernel,
        out_shape=(
            jax.ShapeDtypeStruct((1, TOK, 64), F32),
            jax.ShapeDtypeStruct((1, 2, 4, 64, 96), BF16),
        ),
        in_specs=[pl.BlockSpec(memory_space=pltpu.SMEM)] + [vmem] * 14,
        out_specs=(vmem, vmem),
        scratch_shapes=scratch,
        compiler_params=pltpu.CompilerParams(
            collective_id=0, has_side_effects=True, vmem_limit_bytes=32 * 1024 * 1024
        ),
    )(
        frame_offset, noisy_latent, step_index, query_input, key_input, value_input,
        context_keys, context_values, query_gain.reshape(1, -1), key_gain.reshape(1, -1),
        gate_table, head_weight, conv_weight, conv_bias.reshape(1, -1),
        jnp.asarray(wave_rows()),
    )


def fused_fits(mesh):
    return dict(mesh.shape) == {"block": NB, "seq": NS, "mp": NM}


def solution(mesh):
    return jax.shard_map(
        fused_body if fused_fits(mesh) else body,
        mesh=mesh,
        in_specs=(
            P("block", "seq", None),
            P("block", "seq"),
            P(),
            P("block", "seq", "mp"),
            P("block", "seq", "mp"),
            P("block", "seq", "mp"),
            P("block", "seq", "mp"),
            P("block", "seq", "mp"),
            P("mp"),
            P("mp"),
            P(None, "mp"),
            P("mp", None),
            P(None, None, None, None, "mp"),
            P("mp"),
        ),
        out_specs=(P("block", "seq", None), P("block", None, None, "seq", "mp")),
        check_vma=False,
    )
```

```python
import math

import jax
import jax.numpy as jnp
import numpy as np
from jax import lax
from jax.experimental import pallas as pl
from jax.experimental.pallas import tpu as pltpu
from jax.sharding import PartitionSpec as P

HEADS = 20
HD = 128
LAT = 16
STEPS = 30
FRAMES = 2
PW = 64
RDEV = 2


shift_factor = 8.0


def passed_along(x, axis, by):
    devices = lax.axis_size(axis)
    pairs = [(i, i + by) for i in range(devices) if 0 <= i + by < devices]
    return lax.ppermute(x, axis, pairs)


def padded_2(x, sides, width):
    for axis, dim in sides:
        devices, length = (lax.axis_size(axis), x.shape[dim])
        up = [(i, (i + 1) % devices) for i in range(devices - 1)]
        down = [(j, i) for i, j in up]
        last = lax.slice_in_dim(x, length - width, length, axis=dim)
        initial = lax.slice_in_dim(x, 0, width, axis=dim)
        before = lax.ppermute(last, axis, up)
        after = lax.ppermute(initial, axis, down)
        x = jnp.concatenate([before, x, after], axis=dim)
    return x


def frequency_rows():
    pairs_time = (HD - 4 * (HD // 6)) // 2
    pairs_side = HD // 6
    time_part = 10000.0 ** (-np.arange(pairs_time) / pairs_time)
    side_part = 10000.0 ** (-np.arange(pairs_side) / pairs_side)
    blank_time = np.zeros(pairs_time)
    blank_side = np.zeros(pairs_side)
    along_time = np.concatenate([time_part, blank_side, blank_side])
    along_rows = np.concatenate([blank_time, side_part, blank_side])
    along_cols = np.concatenate([blank_time, blank_side, side_part])
    return (
        jnp.asarray(along_time, jnp.float32),
        jnp.asarray(along_rows, jnp.float32),
        jnp.asarray(along_cols, jnp.float32),
    )


def square_total(raw_input):
    values = raw_input.astype(jnp.float32)
    return jnp.sum(values * values, axis=1)


def normalize_rotate(raw_input, total_sq, gain_row, time_pos, row_pos, col_pos):
    amount = raw_input.shape[0]
    head_count = raw_input.shape[1] // HD
    values = raw_input.astype(jnp.float32).reshape(amount, head_count, HD)
    factor = lax.rsqrt(total_sq / (HEADS * HD) + 1e-06)[:, None, None]
    values = values * factor * gain_row.reshape(1, head_count, HD)
    along_time, along_rows, along_cols = frequency_rows()
    angles = (
        time_pos[:, None] * along_time[None, :]
        + row_pos[:, None] * along_rows[None, :]
        + col_pos[:, None] * along_cols[None, :]
    )
    cosine = jnp.cos(angles)[:, None, :]
    sine_part = jnp.sin(angles)[:, None, :]
    paired = values.reshape(amount, head_count, HD // 2, 2)
    real_part = paired[..., 0]
    imag_part = paired[..., 1]
    turned = jnp.stack(
        [real_part * cosine - imag_part * sine_part, real_part * sine_part + imag_part * cosine],
        axis=-1,
    )
    return turned.reshape(amount, head_count * HD).astype(jnp.bfloat16)


def noise_level(level_now):
    remain = 1.0 - level_now / STEPS
    return shift_factor * remain / (1.0 + (shift_factor - 1.0) * remain)


def lift_tokens(tokens, columns, grid_rows):
    shaped = tokens.reshape(FRAMES, grid_rows, columns, 2, 2, LAT)
    return shaped.transpose(0, 1, 3, 2, 4, 5).reshape(FRAMES, 2 * grid_rows, 2 * columns, LAT)


def convolve(padded, conv_weight, conv_bias):
    frames_out = padded.shape[0] - 2
    height = padded.shape[1] - 2
    span_cols = padded.shape[2] - 2
    pieces = []
    for time_tap in range(3):
        for row_tap in range(3):
            for col_tap in range(3):
                pieces.append(
                    padded[
                        time_tap : time_tap + frames_out,
                        row_tap : row_tap + height,
                        col_tap : col_tap + span_cols,
                        :,
                    ]
                )
    stacked = jnp.stack(pieces, axis=3).reshape(frames_out * height * span_cols, 27 * LAT)
    flat_weight = conv_weight.reshape(27 * LAT, conv_weight.shape[-1])
    summed = jnp.dot(stacked, flat_weight, preferred_element_type=jnp.float32)
    summed = summed + conv_bias[None, :]
    return summed.astype(jnp.bfloat16).reshape(frames_out, height, span_cols, -1)


def with_cache(slab):
    earlier = passed_along(slab, "block", 1)
    return jnp.concatenate([earlier, slab], 0)


def body(
    noisy_latent,
    step_index,
    frame_offset,
    query_input,
    key_input,
    value_input,
    context_keys,
    context_values,
    query_gain,
    key_gain,
    gate_table,
    head_weight,
    conv_weight,
    conv_bias,
):
    clip_pos = lax.axis_index("block")
    seq_pos = lax.axis_index("seq")
    seq_count = lax.axis_size("seq")
    tok_rows = query_input.shape[1]
    ctx_rows = context_keys.shape[1]
    local_width = query_input.shape[2]
    local_heads = local_width // HD
    grid_rows = RDEV * seq_count // FRAMES
    inverse_root = 1.0 / math.sqrt(HD)
    relayed = passed_along(jnp.stack([context_keys[0], context_values[0]]), "block", 1)
    query_sq, key_sq, prior_sq = lax.psum(
        (square_total(query_input[0]), square_total(key_input[0]), square_total(relayed[0])), "mp"
    )
    token_ids = seq_pos * tok_rows + jnp.arange(tok_rows, dtype=jnp.int32)
    frame_ids = token_ids // (grid_rows * PW)
    row_ids = (token_ids // PW % grid_rows).astype(jnp.float32)
    col_ids = (token_ids % PW).astype(jnp.float32)
    own_offset = lax.dynamic_index_in_dim(frame_offset, clip_pos, 0, keepdims=False)
    prior_offset = lax.dynamic_index_in_dim(
        frame_offset, jnp.maximum(clip_pos - 1, 0), 0, keepdims=False
    )
    moment = (own_offset + frame_ids).astype(jnp.float32)
    queries = normalize_rotate(query_input[0], query_sq, query_gain, moment, row_ids, col_ids)
    own_keys = normalize_rotate(key_input[0], key_sq, key_gain, moment, row_ids, col_ids)
    own_values = value_input[0]
    context_ids = seq_pos * ctx_rows + jnp.arange(ctx_rows, dtype=jnp.int32)
    context_moment = jnp.zeros((ctx_rows,), jnp.float32) + (prior_offset + FRAMES - 1).astype(
        jnp.float32
    )
    prior_rot = normalize_rotate(
        relayed[0],
        prior_sq,
        key_gain,
        context_moment,
        (context_ids // PW).astype(jnp.float32),
        (context_ids % PW).astype(jnp.float32),
    )
    prior_values = relayed[1]
    keep_prior = (clip_pos > 0).astype(jnp.float32)
    start_state = (
        jnp.zeros((tok_rows, local_width), jnp.float32),
        jnp.zeros((tok_rows, local_heads), jnp.float32),
    )
    joint_rows = tok_rows + ctx_rows
    joint_keys = jnp.concatenate([own_keys, prior_rot], 0)
    joint_values = jnp.concatenate([own_values, prior_values], 0)
    piece = (
        lax.all_gather(joint_keys, "seq", axis=0, tiled=True),
        lax.all_gather(joint_values, "seq", axis=0, tiled=True),
    )
    local_rows = jnp.arange(piece[0].shape[0], dtype=jnp.int32) % joint_rows
    row_keep = jnp.where(local_rows < tok_rows, 1.0, keep_prior)
    key_piece = piece[0]
    value_piece = piece[1]

    def per_head(head_slot, state):
        numer, denom = state
        query_head = lax.dynamic_slice_in_dim(queries, head_slot * HD, HD, 1)
        key_head = lax.dynamic_slice_in_dim(key_piece, head_slot * HD, HD, 1)
        value_head = lax.dynamic_slice_in_dim(value_piece, head_slot * HD, HD, 1)
        scores = (
            jnp.einsum("qd,kd->qk", query_head, key_head, preferred_element_type=jnp.float32)
            * inverse_root
        )
        expon = jnp.exp(scores) * row_keep[None, :]
        added = jnp.dot(expon.astype(jnp.bfloat16), value_head, preferred_element_type=jnp.float32)
        old_numer = lax.dynamic_slice_in_dim(numer, head_slot * HD, HD, 1)
        numer = lax.dynamic_update_slice_in_dim(numer, old_numer + added, head_slot * HD, 1)
        old_denom = lax.dynamic_slice_in_dim(denom, head_slot, 1, 1)
        denom = lax.dynamic_update_slice_in_dim(
            denom, old_denom + jnp.sum(expon, axis=1, keepdims=True), head_slot, 1
        )
        return (numer, denom)

    state = lax.fori_loop(0, local_heads, per_head, start_state)
    numer, denom = state
    attention = (numer.reshape(tok_rows, local_heads, HD) / denom[:, :, None]).reshape(
        tok_rows, local_width
    )
    one_hot = (step_index[0][:, None] == jnp.arange(STEPS, dtype=jnp.int32)[None, :]).astype(
        jnp.float32
    )
    gate_rows = jnp.dot(one_hot, gate_table, precision=lax.Precision.HIGHEST)
    gated_out = (attention * gate_rows).astype(jnp.bfloat16)
    partial_sum = jnp.dot(gated_out, head_weight, preferred_element_type=jnp.float32)
    velocity = lax.psum(partial_sum, "mp")
    level_now = step_index[0].astype(jnp.float32)
    now_sigma = noise_level(level_now)[:, None]
    next_sigma = noise_level(level_now + 1.0)[:, None]
    latent_now = noisy_latent[0]
    next_latent = latent_now + (next_sigma - now_sigma) * velocity
    clean_tokens = (latent_now - now_sigma * velocity).astype(jnp.bfloat16)
    slab_cols = PW // seq_count
    rows_local = clean_tokens.reshape(RDEV, PW, clean_tokens.shape[1])
    moved = lax.all_to_all(rows_local, "seq", split_axis=1, concat_axis=0, tiled=True)
    slab = lift_tokens(moved, slab_cols, grid_rows)
    framed = padded_2(with_cache(slab), (("seq", 2),), 1)
    framed = jnp.pad(framed, ((0, 0), (1, 1), (0, 0), (0, 0)))
    decoded = convolve(framed, conv_weight, conv_bias)
    return (next_latent[None], decoded[None])


def wave_rows():
    pairs_side = HD // 6
    pairs_time = (HD - 4 * pairs_side) // 2
    table = np.zeros((8, HD), np.float32)
    for lane in range(HD):
        pair = lane // 2
        if pair < pairs_time:
            table[0, lane] = np.float32(10000.0 ** (-pair / pairs_time))
        elif pair < pairs_time + pairs_side:
            table[1, lane] = np.float32(10000.0 ** (-(pair - pairs_time) / pairs_side))
        else:
            table[2, lane] = np.float32(10000.0 ** (-(pair - pairs_time - pairs_side) / pairs_side))
            table[3, lane] = 1.0
    return table


MESH = pl.DeviceIdType.MESH
F32 = jnp.float32
BF16 = jnp.bfloat16
NB, NS, NM = 4, 2, 4
TOK, CTXR, WID, NH = 128, 64, 640, 5
KEYS = TOK + CTXR


def dot(a, b):
    return lax.dot_general(a, b, (((1,), (0,)), ((), ())), preferred_element_type=F32)


def dot_nt(a, b):
    return lax.dot_general(a, b, (((1,), (1,)), ((), ())), preferred_element_type=F32)


def dot_tn(a, b):
    return lax.dot_general(a, b, (((0,), (0,)), ((), ())), preferred_element_type=F32)


def step_kernel(
    fo_hbm, noisy_hbm, step_hbm, q_hbm, k_hbm, v_hbm, ck_hbm, cv_hbm, qg_hbm, kg_hbm, gate_hbm,
    hw_hbm, cw_hbm, cb_hbm, waves_hbm,
    next_out, dec_out,
    fo, noisy, step, q_in, k_in, v_in, ck_in, qg, kg, gate, wt, cw, cb, waves, in_sem,
    qall, kbuf, vctx, ckrot, vt, ebuf, numer, st_own, st_prev, dmine, dother, gatet,
    part, rs, nl, lp, nz, sig_now, sig_step, wbig, fr, stage,
    q_send, q_recv, c_send, c_recv, s_send, s_recv, sp_recv, d_send, d_recv,
    r_send, r_recv, n_send, n_recv, l_send, l_recv,
):
    b = lax.axis_index("block")
    s = lax.axis_index("seq")
    m = lax.axis_index("mp")
    nb = lax.rem(b + 1, NB)
    pb = lax.rem(b + NB - 1, NB)
    other = 1 - s

    barrier = pltpu.get_barrier_semaphore()
    for ds in range(NS):
        for dm in range(NM):
            ss, mm = lax.rem(s + ds, NS), lax.rem(m + dm, NM)
            if ds or dm:
                pl.semaphore_signal(barrier, inc=1, device_id=(b, ss, mm), device_id_type=MESH)
            pl.semaphore_signal(barrier, inc=1, device_id=(pb, ss, mm), device_id_type=MESH)

    loads = {}
    for i, (name, src, dst) in enumerate((
        ("fo", fo_hbm, fo), ("waves", waves_hbm, waves), ("q", q_hbm, q_in), ("qg", qg_hbm, qg),
        ("ck", ck_hbm, ck_in), ("kg", kg_hbm, kg), ("k", k_hbm, k_in), ("step", step_hbm, step),
        ("v", v_hbm, v_in), ("cw", cw_hbm, cw), ("gate", gate_hbm, gate), ("wt", hw_hbm, wt),
        ("noisy", noisy_hbm, noisy), ("cb", cb_hbm, cb),
    )):
        loads[name] = pltpu.make_async_copy(src, dst, in_sem.at[i])
        loads[name].start()

    lane = lax.broadcasted_iota(jnp.int32, (8, HD), 1)
    even = lax.rem(lane, 2) == 0
    sign = jnp.where(even, -1.0, 1.0)[0:1]
    row8 = lax.broadcasted_iota(jnp.int32, (8, HD), 0)
    loads["fo"].wait()
    loads["waves"].wait()
    base = fo[b]
    tau = jnp.where(row8 == 2, base + 1, base + s).astype(F32)
    hpos = jnp.where(row8 == 2, s, jnp.where(row8 == 1, 1, 0)).astype(F32)
    ang = tau * waves[0:1] + hpos * waves[1:2]
    cos_r, sin_r = jnp.cos(ang), jnp.sin(ang)
    wpos = lax.broadcasted_iota(jnp.int32, (64, HD), 0).astype(F32)
    ang_c = wpos * waves[2:3]
    cos_c, sin_c = jnp.cos(ang_c), jnp.sin(ang_c)
    col_lane = jnp.broadcast_to(waves[3:4], (64, HD)) > 0.5

    def table(r):
        c = jnp.where(col_lane, cos_c, jnp.broadcast_to(cos_r[r : r + 1], (64, HD)))
        n = jnp.where(col_lane, sin_c, jnp.broadcast_to(sin_r[r : r + 1], (64, HD)))
        return c, n * sign

    c0, n0 = table(0)
    c1, n1 = table(1)
    cos_t = jnp.concatenate([c0, c1], 0)
    sin_t = jnp.concatenate([n0, n1], 0)
    cos_x, sin_x = table(2)

    pr = lax.broadcasted_iota(jnp.int32, (HD, HD), 0)
    pc = lax.broadcasted_iota(jnp.int32, (HD, HD), 1)
    swap = jnp.where(pc == pr + 1 - 2 * lax.rem(pr, 2), 1.0, 0.0).astype(BF16)

    def swapped(g):
        g8 = jnp.broadcast_to(g, (8, HD))
        return jnp.where(even, pltpu.roll(g8, HD - 1, 1), pltpu.roll(g8, 1, 1))[0:1]

    def rotated(x_ref, gain, ct, st, store):
        total = None
        for h in range(NH):
            sl = slice(h * HD, (h + 1) * HD)
            xb = x_ref[0, :, sl]
            x = xb.astype(F32)
            g = gain[h : h + 1]
            xs = dot(xb, swap)
            store(sl, ((x * g) * ct + (xs * swapped(g)) * st).astype(BF16))
            total = x * x if total is None else total + x * x
        return total

    def store_q(sl, val):
        qall[s, :, sl] = val

    def store_k(sl, val):
        kbuf[0:TOK, sl] = val

    def store_c(sl, val):
        ckrot[:, sl] = val

    loads["q"].wait()
    loads["qg"].wait()
    sq_q = rotated(q_in, qg, cos_t, sin_t, store_q)
    loads["ck"].wait()
    loads["kg"].wait()
    sq_c = rotated(ck_in, kg, cos_x, sin_x, store_c)
    loads["k"].wait()
    sq_k = rotated(k_in, kg, cos_t, sin_t, store_k)
    row_q = jnp.sum(sq_q.T, axis=0, keepdims=True)
    row_k = jnp.sum(sq_k.T, axis=0, keepdims=True)
    sq_c2 = jnp.concatenate([sq_c, jnp.zeros((64, HD), F32)], 0)
    row_c = jnp.sum(sq_c2.T, axis=0, keepdims=True)
    loads["step"].wait()
    step_row = step[...].astype(F32)
    st_own[s, m] = jnp.where(
        row8 == 0, row_q, jnp.where(row8 == 1, row_k, jnp.where(row8 == 2, row_c, step_row))
    )

    pl.semaphore_wait(barrier, 2 * NS * NM - 1)

    def remote(src, dst, send, recv, dev):
        return pltpu.make_async_remote_copy(
            src_ref=src, dst_ref=dst, send_sem=send, recv_sem=recv, device_id=dev,
            device_id_type=MESH,
        )

    pend = []

    def go(*args):
        copy = remote(*args)
        copy.start()
        pend.append(copy)

    i = 0
    for ds in range(NS):
        for dm in range(NM):
            ss, mm = lax.rem(s + ds, NS), lax.rem(m + dm, NM)
            if ds or dm:
                go(st_own.at[s, m], st_own.at[s, m], s_send.at[i], s_recv.at[s, m], (b, ss, mm))
                i += 1
    for dm in range(NM):
        mm = lax.rem(m + dm, NM)
        go(st_own.at[s, m], st_prev.at[m], s_send.at[i], sp_recv.at[m], (nb, s, mm))
        i += 1

    for h in range(NH):
        hl = pl.ds(h * HD, HD)
        go(qall.at[s, :, hl], qall.at[s, :, hl], q_send.at[h], q_recv.at[h], (b, other, m))
        go(ckrot.at[:, hl], kbuf.at[pl.ds(TOK, CTXR), hl], c_send.at[h], c_recv.at[h], (nb, s, m))
    go(cv_hbm.at[0], vctx, c_send.at[NH], c_recv.at[NH], (nb, s, m))

    loads["v"].wait()
    for h in range(NH):
        sl = slice(h * HD, (h + 1) * HD)
        vt[sl, 0:TOK] = v_in[0, :, sl].astype(F32).T.astype(BF16)
    steps_col = jnp.broadcast_to(step_row, (HD, HD)).T
    lane64 = lax.broadcasted_iota(jnp.int32, (64, HD), 1)
    steps2 = jnp.where(lane64 < 64, steps_col[0:64], steps_col[64:128])
    loads["noisy"].wait()
    t = jnp.concatenate([noisy[0], jnp.zeros((64, HD), F32)], 0).T
    nz[...] = jnp.concatenate([t[0:64, 0:64], t[64:128, 0:64]], 1)

    def level(at):
        remain = 1.0 - at / STEPS
        return 8.0 * remain / (1.0 + 7.0 * remain)

    now = level(steps2)
    sig_now[...] = now
    sig_step[...] = level(steps2 + 1.0) - now
    lp[:, :, 0:16, :] = jnp.zeros((2, 2, 16, HD), BF16)
    lp[:, :, 80:96, :] = jnp.zeros((2, 2, 16, HD), BF16)
    wbig[...] = jnp.zeros(wbig.shape, BF16)
    loads["cw"].wait()
    for qo in range(2):
        for a in range(3):
            for j in range(2):
                for qi in range(2):
                    d = qo + 2 * j + qi - 1
                    if not 0 <= d <= 2:
                        continue
                    for y in range(4):
                        for yo in range(4):
                            t = y - yo + 1
                            if not 0 <= t <= 2:
                                continue
                            r = a * 256 + j * 128 + y * 32 + qi * 16
                            wbig[qo, r : r + 16, yo * 128 : yo * 128 + 96] = cw[a, t, d]

    for ds in range(NS):
        for dm in range(NM):
            if ds or dm:
                ss, mm = lax.rem(s + ds, NS), lax.rem(m + dm, NM)
                remote(st_own.at[ss, mm], st_own.at[ss, mm], s_send.at[0], s_recv.at[ss, mm],
                       (b, other, m)).wait_recv()
    for mm in range(NM):
        remote(st_prev.at[mm], st_prev.at[mm], s_send.at[0], sp_recv.at[mm],
               (b, other, m)).wait_recv()
    inv = 1.0 / (HEADS * HD)
    qstat = [st_own[e, 0] + st_own[e, 1] + st_own[e, 2] + st_own[e, 3] for e in range(NS)]
    kstat = st_own[s, 0] + st_own[s, 1] + st_own[s, 2] + st_own[s, 3]
    cstat = st_prev[0] + st_prev[1] + st_prev[2] + st_prev[3]
    scale = 1.4426950408889634 / math.sqrt(HD)
    fq = [lax.rsqrt(x[0:1] * inv + 1e-06) * scale for x in qstat]
    fk_own = jnp.broadcast_to(lax.rsqrt(kstat[1:2] * inv + 1e-06), (HD, HD)).T
    fk_ctx = jnp.broadcast_to(lax.rsqrt(cstat[2:3] * inv + 1e-06), (HD, HD)).T[0:CTXR]
    fk = jnp.concatenate([fk_own, fk_ctx], 0)
    factor = jnp.concatenate([fk * fq[0], fk * fq[1]], 1)

    steps_all = jnp.concatenate([st_own[0, 0][3:4], st_own[1, 0][3:4]], 1)
    which = lax.broadcasted_iota(jnp.int32, (STEPS, 2 * TOK), 0).astype(F32)
    hot = jnp.where(which == steps_all, 1.0, 0.0).astype(BF16)
    loads["gate"].wait()
    g_all = gate[...]
    g_hi = g_all.astype(BF16)
    g_lo = (g_all - g_hi.astype(F32)).astype(BF16)
    gatet[...] = dot_tn(g_hi, hot) + dot_tn(g_lo, hot)

    has_prior = jnp.broadcast_to(b, (CTXR, 2 * TOK)) > 0
    sub = lax.broadcasted_iota(jnp.int32, (8, 2 * TOK), 0)
    sums = jnp.ones((8, 2 * TOK), F32)
    for h in range(NH):
        sl = slice(h * HD, (h + 1) * HD)
        hl = pl.ds(h * HD, HD)
        remote(qall.at[s, :, hl], qall.at[other, :, hl], q_send.at[h], q_recv.at[h],
               (b, other, m)).wait_recv()
        remote(ckrot.at[:, hl], kbuf.at[pl.ds(TOK, CTXR), hl], c_send.at[h], c_recv.at[h],
               (b, other, m)).wait_recv()
        qh = jnp.concatenate([qall[0, :, sl], qall[1, :, sl]], 0)
        sc = dot_nt(kbuf[:, sl], qh) * factor
        e = jnp.exp2(sc)
        e_own = e[0:TOK]
        e_ctx = jnp.where(has_prior, e[TOK:KEYS], 0.0)
        den = jnp.sum(e_own, axis=0, keepdims=True) + jnp.sum(e_ctx, axis=0, keepdims=True)
        sums = jnp.where(sub == h, den, sums)
        ebuf[h, 0:TOK] = e_own.astype(BF16)
        ebuf[h, TOK:KEYS] = e_ctx.astype(BF16)
    dmine[...] = sums
    go(dmine, dother, d_send, d_recv, (b, other, m))
    remote(vctx, vctx, c_send.at[NH], c_recv.at[NH], (b, other, m)).wait_recv()
    for h in range(NH):
        sl = slice(h * HD, (h + 1) * HD)
        vt[sl, TOK:KEYS] = vctx[:, sl].astype(F32).T.astype(BF16)
    for h in range(NH):
        sl = slice(h * HD, (h + 1) * HD)
        numer[sl] = dot(vt[sl, :], ebuf[h]) * gatet[sl]
    remote(dmine, dother, d_send, d_recv, (b, other, m)).wait_recv()
    recip = 1.0 / (dmine[...] + dother[...])
    loads["wt"].wait()
    vel_t = jnp.zeros((64, 2 * TOK), F32)
    for h in range(NH):
        sl = slice(h * HD, (h + 1) * HD)
        vel_t += dot(wt[:, sl], (numer[sl] * recip[h : h + 1]).astype(BF16))
    for f in range(2):
        t = jnp.concatenate([vel_t[:, f * TOK : (f + 1) * TOK], jnp.zeros((64, HD), F32)], 0).T
        part[f] = jnp.concatenate([t[0:64, 0:64], t[64:128, 0:64]], 1)

    def cols(mm):
        return pl.ds(pl.multiple_of(mm * 16, 16), 16)

    def lcols(mm):
        return pl.ds(pl.multiple_of(mm * 16 + 16, 16), 16)

    i = 0
    for ds in range(NS):
        for dm in range(NM):
            if ds or dm:
                ss, mm = lax.rem(s + ds, NS), lax.rem(m + dm, NM)
                go(part.at[ss, cols(mm)], rs.at[s, m], r_send.at[i], r_recv.at[s, m], (b, ss, mm))
                i += 1
    rs[s, m] = part[s, cols(m)]
    for ds in range(NS):
        for dm in range(NM):
            if ds or dm:
                ss, mm = lax.rem(s + ds, NS), lax.rem(m + dm, NM)
                remote(rs.at[ss, mm], rs.at[ss, mm], r_send.at[0], r_recv.at[ss, mm],
                       (b, other, m)).wait_recv()
    vel = rs[0, 0]
    for e in range(1, NS * NM):
        vel = vel + rs[e // NM, e % NM]
    latent = nz[cols(m), :]
    lp[1, s, lcols(m), :] = (latent - sig_now[cols(m), :] * vel).astype(BF16)
    mine = lp.at[1, s, lcols(m)]
    i = 0
    for ds in range(NS):
        for dm in range(NM):
            ss, mm = lax.rem(s + ds, NS), lax.rem(m + dm, NM)
            go(mine, lp.at[0, s, lcols(m)], l_send.at[i], l_recv.at[0, s, m], (nb, ss, mm))
            i += 1
            if ds or dm:
                go(mine, mine, l_send.at[i], l_recv.at[1, s, m], (b, ss, mm))
                i += 1
    nl[cols(m), :] = latent + sig_step[cols(m), :] * vel
    for dm in range(1, NM):
        mm = lax.rem(m + dm, NM)
        go(nl.at[cols(m)], nl.at[cols(m)], n_send.at[dm - 1], n_recv.at[m], (b, s, mm))

    for c in (1, 0):
        for ds in range(NS):
            for dm in range(NM):
                if c == 0 or ds or dm:
                    ss, mm = lax.rem(s + ds, NS), lax.rem(m + dm, NM)
                    at = lp.at[c, ss, lcols(mm)]
                    remote(at, at, l_send.at[0], l_recv.at[c, ss, mm], (b, other, m)).wait_recv()
    slab = pl.ds(pl.multiple_of(s * 32, 32), 64)
    prior2 = jnp.broadcast_to(b, (64, HD)) > 0
    for f in range(2):
        fr[f] = jnp.where(prior2, lp[0, f, slab, :].astype(F32), 0.0)
        fr[2 + f] = lp[1, f, slab, :].astype(F32)
    loads["cb"].wait()
    bias = cb[...]
    for qo in range(2):
        rows = []
        for t in range(2):
            taps = []
            for a in range(3):
                for j in range(2):
                    taps.append(fr[t + a, 15 + qo + j : 47 + qo + j, :].astype(BF16))
            rows.append(jnp.concatenate(taps, 1))
        res = dot(jnp.concatenate(rows, 0), wbig[qo])
        for t in range(2):
            for y in range(4):
                stage[t * 4 + y, pl.ds(qo, 32, stride=2), :] = res[
                    t * 32 : (t + 1) * 32, y * 128 : (y + 1) * 128
                ]
    for t in range(2):
        for y in range(4):
            dec_out[0, t, y] = (stage[t * 4 + y][:, 0:96] + bias).astype(BF16)

    for dm in range(1, NM):
        mm = lax.rem(m + dm, NM)
        remote(nl.at[cols(mm)], nl.at[cols(mm)], n_send.at[0], n_recv.at[mm],
               (b, other, m)).wait_recv()
    final = jnp.concatenate([nl[...], jnp.zeros((64, HD), F32)], 0).T
    next_out[0] = jnp.concatenate([final[0:64, 0:64], final[64:128, 0:64]], 1)
    for copy in pend:
        copy.wait_send()


def fused_body(
    noisy_latent, step_index, frame_offset, query_input, key_input, value_input, context_keys,
    context_values, query_gain, key_gain, gate_table, head_weight, conv_weight, conv_bias,
):
    vmem = pl.BlockSpec(memory_space=pltpu.VMEM)
    dma = pltpu.SemaphoreType.DMA
    scratch = [
        pltpu.SMEM((4,), jnp.int32),
        pltpu.VMEM((1, 64, TOK), F32),
        pltpu.VMEM((1, TOK), jnp.int32),
        pltpu.VMEM((1, TOK, WID), BF16),
        pltpu.VMEM((1, TOK, WID), BF16),
        pltpu.VMEM((1, TOK, WID), BF16),
        pltpu.VMEM((1, CTXR, WID), BF16),
        pltpu.VMEM((NH, HD), F32),
        pltpu.VMEM((NH, HD), F32),
        pltpu.VMEM((STEPS, WID), F32),
        pltpu.VMEM((64, WID), BF16),
        pltpu.VMEM((3, 3, 3, LAT, 96), BF16),
        pltpu.VMEM((1, 96), F32),
        pltpu.VMEM((8, HD), F32),
        dma((14,)),
        pltpu.VMEM((2, TOK, WID), BF16),
        pltpu.VMEM((KEYS, WID), BF16),
        pltpu.VMEM((CTXR, WID), BF16),
        pltpu.VMEM((CTXR, WID), BF16),
        pltpu.VMEM((WID, KEYS), BF16),
        pltpu.VMEM((NH, KEYS, 2 * TOK), BF16),
        pltpu.VMEM((WID, 2 * TOK), F32),
        pltpu.VMEM((NS, NM, 8, HD), F32),
        pltpu.VMEM((NM, 8, HD), F32),
        pltpu.VMEM((8, 2 * TOK), F32),
        pltpu.VMEM((8, 2 * TOK), F32),
        pltpu.VMEM((WID, 2 * TOK), F32),
        pltpu.VMEM((2, 64, HD), F32),
        pltpu.VMEM((NS, NM, 16, HD), F32),
        pltpu.VMEM((64, HD), F32),
        pltpu.VMEM((2, 2, 96, HD), BF16),
        pltpu.VMEM((64, HD), F32),
        pltpu.VMEM((64, HD), F32),
        pltpu.VMEM((64, HD), F32),
        pltpu.VMEM((2, 768, 512), BF16),
        pltpu.VMEM((4, 64, HD), F32),
        pltpu.VMEM((8, 64, HD), F32),
        dma((NH,)), dma((NH,)), dma((NH + 1,)), dma((NH + 1,)),
        dma((11,)), dma((NS, NM)), dma((NM,)),
        dma, dma,
        dma((7,)), dma((NS, NM)),
        dma((3,)), dma((NM,)),
        dma((15,)), dma((2, NS, NM)),
    ]
    hbm = pl.BlockSpec(memory_space=pltpu.HBM)
    next_latent, decoded = pl.pallas_call(
        step_kernel,
        out_shape=(
            jax.ShapeDtypeStruct((1, 64, TOK), F32),
            jax.ShapeDtypeStruct((1, 2, 4, 64, 96), BF16),
        ),
        in_specs=[hbm] * 15,
        out_specs=(vmem, vmem),
        scratch_shapes=scratch,
        compiler_params=pltpu.CompilerParams(
            collective_id=0, has_side_effects=True, vmem_limit_bytes=60 * 1024 * 1024
        ),
    )(
        frame_offset, noisy_latent.transpose(0, 2, 1), step_index, query_input, key_input, value_input,
        context_keys, context_values, query_gain.reshape(NH, HD), key_gain.reshape(NH, HD),
        gate_table, head_weight.T, conv_weight, conv_bias.reshape(1, -1),
        jnp.asarray(wave_rows()),
    )
    return next_latent.transpose(0, 2, 1), decoded


def fused_fits(mesh):
    return dict(mesh.shape) == {"block": NB, "seq": NS, "mp": NM}


def solution(mesh):
    return jax.shard_map(
        fused_body if fused_fits(mesh) else body,
        mesh=mesh,
        in_specs=(
            P("block", "seq", None),
            P("block", "seq"),
            P(),
            P("block", "seq", "mp"),
            P("block", "seq", "mp"),
            P("block", "seq", "mp"),
            P("block", "seq", "mp"),
            P("block", "seq", "mp"),
            P("mp"),
            P("mp"),
            P(None, "mp"),
            P("mp", None),
            P(None, None, None, None, "mp"),
            P("mp"),
        ),
        out_specs=(P("block", "seq", None), P("block", None, None, "seq", "mp")),
        check_vma=False,
    )
```

```python
import math

import jax
import jax.numpy as jnp
import numpy as np
from jax import lax
from jax.experimental import pallas as pl
from jax.experimental.pallas import tpu as pltpu
from jax.sharding import PartitionSpec as P

HEADS = 20
HD = 128
LAT = 16
STEPS = 30
FRAMES = 2
PW = 64
RDEV = 2


shift_factor = 8.0


def passed_along(x, axis, by):
    devices = lax.axis_size(axis)
    pairs = [(i, i + by) for i in range(devices) if 0 <= i + by < devices]
    return lax.ppermute(x, axis, pairs)


def padded_2(x, sides, width):
    for axis, dim in sides:
        devices, length = (lax.axis_size(axis), x.shape[dim])
        up = [(i, (i + 1) % devices) for i in range(devices - 1)]
        down = [(j, i) for i, j in up]
        last = lax.slice_in_dim(x, length - width, length, axis=dim)
        initial = lax.slice_in_dim(x, 0, width, axis=dim)
        before = lax.ppermute(last, axis, up)
        after = lax.ppermute(initial, axis, down)
        x = jnp.concatenate([before, x, after], axis=dim)
    return x


def frequency_rows():
    pairs_time = (HD - 4 * (HD // 6)) // 2
    pairs_side = HD // 6
    time_part = 10000.0 ** (-np.arange(pairs_time) / pairs_time)
    side_part = 10000.0 ** (-np.arange(pairs_side) / pairs_side)
    blank_time = np.zeros(pairs_time)
    blank_side = np.zeros(pairs_side)
    along_time = np.concatenate([time_part, blank_side, blank_side])
    along_rows = np.concatenate([blank_time, side_part, blank_side])
    along_cols = np.concatenate([blank_time, blank_side, side_part])
    return (
        jnp.asarray(along_time, jnp.float32),
        jnp.asarray(along_rows, jnp.float32),
        jnp.asarray(along_cols, jnp.float32),
    )


def square_total(raw_input):
    values = raw_input.astype(jnp.float32)
    return jnp.sum(values * values, axis=1)


def normalize_rotate(raw_input, total_sq, gain_row, time_pos, row_pos, col_pos):
    amount = raw_input.shape[0]
    head_count = raw_input.shape[1] // HD
    values = raw_input.astype(jnp.float32).reshape(amount, head_count, HD)
    factor = lax.rsqrt(total_sq / (HEADS * HD) + 1e-06)[:, None, None]
    values = values * factor * gain_row.reshape(1, head_count, HD)
    along_time, along_rows, along_cols = frequency_rows()
    angles = (
        time_pos[:, None] * along_time[None, :]
        + row_pos[:, None] * along_rows[None, :]
        + col_pos[:, None] * along_cols[None, :]
    )
    cosine = jnp.cos(angles)[:, None, :]
    sine_part = jnp.sin(angles)[:, None, :]
    paired = values.reshape(amount, head_count, HD // 2, 2)
    real_part = paired[..., 0]
    imag_part = paired[..., 1]
    turned = jnp.stack(
        [real_part * cosine - imag_part * sine_part, real_part * sine_part + imag_part * cosine],
        axis=-1,
    )
    return turned.reshape(amount, head_count * HD).astype(jnp.bfloat16)


def noise_level(level_now):
    remain = 1.0 - level_now / STEPS
    return shift_factor * remain / (1.0 + (shift_factor - 1.0) * remain)


def lift_tokens(tokens, columns, grid_rows):
    shaped = tokens.reshape(FRAMES, grid_rows, columns, 2, 2, LAT)
    return shaped.transpose(0, 1, 3, 2, 4, 5).reshape(FRAMES, 2 * grid_rows, 2 * columns, LAT)


def convolve(padded, conv_weight, conv_bias):
    frames_out = padded.shape[0] - 2
    height = padded.shape[1] - 2
    span_cols = padded.shape[2] - 2
    pieces = []
    for time_tap in range(3):
        for row_tap in range(3):
            for col_tap in range(3):
                pieces.append(
                    padded[
                        time_tap : time_tap + frames_out,
                        row_tap : row_tap + height,
                        col_tap : col_tap + span_cols,
                        :,
                    ]
                )
    stacked = jnp.stack(pieces, axis=3).reshape(frames_out * height * span_cols, 27 * LAT)
    flat_weight = conv_weight.reshape(27 * LAT, conv_weight.shape[-1])
    summed = jnp.dot(stacked, flat_weight, preferred_element_type=jnp.float32)
    summed = summed + conv_bias[None, :]
    return summed.astype(jnp.bfloat16).reshape(frames_out, height, span_cols, -1)


def with_cache(slab):
    earlier = passed_along(slab, "block", 1)
    return jnp.concatenate([earlier, slab], 0)


def body(
    noisy_latent,
    step_index,
    frame_offset,
    query_input,
    key_input,
    value_input,
    context_keys,
    context_values,
    query_gain,
    key_gain,
    gate_table,
    head_weight,
    conv_weight,
    conv_bias,
):
    clip_pos = lax.axis_index("block")
    seq_pos = lax.axis_index("seq")
    seq_count = lax.axis_size("seq")
    tok_rows = query_input.shape[1]
    ctx_rows = context_keys.shape[1]
    local_width = query_input.shape[2]
    local_heads = local_width // HD
    grid_rows = RDEV * seq_count // FRAMES
    inverse_root = 1.0 / math.sqrt(HD)
    relayed = passed_along(jnp.stack([context_keys[0], context_values[0]]), "block", 1)
    query_sq, key_sq, prior_sq = lax.psum(
        (square_total(query_input[0]), square_total(key_input[0]), square_total(relayed[0])), "mp"
    )
    token_ids = seq_pos * tok_rows + jnp.arange(tok_rows, dtype=jnp.int32)
    frame_ids = token_ids // (grid_rows * PW)
    row_ids = (token_ids // PW % grid_rows).astype(jnp.float32)
    col_ids = (token_ids % PW).astype(jnp.float32)
    own_offset = lax.dynamic_index_in_dim(frame_offset, clip_pos, 0, keepdims=False)
    prior_offset = lax.dynamic_index_in_dim(
        frame_offset, jnp.maximum(clip_pos - 1, 0), 0, keepdims=False
    )
    moment = (own_offset + frame_ids).astype(jnp.float32)
    queries = normalize_rotate(query_input[0], query_sq, query_gain, moment, row_ids, col_ids)
    own_keys = normalize_rotate(key_input[0], key_sq, key_gain, moment, row_ids, col_ids)
    own_values = value_input[0]
    context_ids = seq_pos * ctx_rows + jnp.arange(ctx_rows, dtype=jnp.int32)
    context_moment = jnp.zeros((ctx_rows,), jnp.float32) + (prior_offset + FRAMES - 1).astype(
        jnp.float32
    )
    prior_rot = normalize_rotate(
        relayed[0],
        prior_sq,
        key_gain,
        context_moment,
        (context_ids // PW).astype(jnp.float32),
        (context_ids % PW).astype(jnp.float32),
    )
    prior_values = relayed[1]
    keep_prior = (clip_pos > 0).astype(jnp.float32)
    start_state = (
        jnp.zeros((tok_rows, local_width), jnp.float32),
        jnp.zeros((tok_rows, local_heads), jnp.float32),
    )
    joint_rows = tok_rows + ctx_rows
    joint_keys = jnp.concatenate([own_keys, prior_rot], 0)
    joint_values = jnp.concatenate([own_values, prior_values], 0)
    piece = (
        lax.all_gather(joint_keys, "seq", axis=0, tiled=True),
        lax.all_gather(joint_values, "seq", axis=0, tiled=True),
    )
    local_rows = jnp.arange(piece[0].shape[0], dtype=jnp.int32) % joint_rows
    row_keep = jnp.where(local_rows < tok_rows, 1.0, keep_prior)
    key_piece = piece[0]
    value_piece = piece[1]

    def per_head(head_slot, state):
        numer, denom = state
        query_head = lax.dynamic_slice_in_dim(queries, head_slot * HD, HD, 1)
        key_head = lax.dynamic_slice_in_dim(key_piece, head_slot * HD, HD, 1)
        value_head = lax.dynamic_slice_in_dim(value_piece, head_slot * HD, HD, 1)
        scores = (
            jnp.einsum("qd,kd->qk", query_head, key_head, preferred_element_type=jnp.float32)
            * inverse_root
        )
        expon = jnp.exp(scores) * row_keep[None, :]
        added = jnp.dot(expon.astype(jnp.bfloat16), value_head, preferred_element_type=jnp.float32)
        old_numer = lax.dynamic_slice_in_dim(numer, head_slot * HD, HD, 1)
        numer = lax.dynamic_update_slice_in_dim(numer, old_numer + added, head_slot * HD, 1)
        old_denom = lax.dynamic_slice_in_dim(denom, head_slot, 1, 1)
        denom = lax.dynamic_update_slice_in_dim(
            denom, old_denom + jnp.sum(expon, axis=1, keepdims=True), head_slot, 1
        )
        return (numer, denom)

    state = lax.fori_loop(0, local_heads, per_head, start_state)
    numer, denom = state
    attention = (numer.reshape(tok_rows, local_heads, HD) / denom[:, :, None]).reshape(
        tok_rows, local_width
    )
    one_hot = (step_index[0][:, None] == jnp.arange(STEPS, dtype=jnp.int32)[None, :]).astype(
        jnp.float32
    )
    gate_rows = jnp.dot(one_hot, gate_table, precision=lax.Precision.HIGHEST)
    gated_out = (attention * gate_rows).astype(jnp.bfloat16)
    partial_sum = jnp.dot(gated_out, head_weight, preferred_element_type=jnp.float32)
    velocity = lax.psum(partial_sum, "mp")
    level_now = step_index[0].astype(jnp.float32)
    now_sigma = noise_level(level_now)[:, None]
    next_sigma = noise_level(level_now + 1.0)[:, None]
    latent_now = noisy_latent[0]
    next_latent = latent_now + (next_sigma - now_sigma) * velocity
    clean_tokens = (latent_now - now_sigma * velocity).astype(jnp.bfloat16)
    slab_cols = PW // seq_count
    rows_local = clean_tokens.reshape(RDEV, PW, clean_tokens.shape[1])
    moved = lax.all_to_all(rows_local, "seq", split_axis=1, concat_axis=0, tiled=True)
    slab = lift_tokens(moved, slab_cols, grid_rows)
    framed = padded_2(with_cache(slab), (("seq", 2),), 1)
    framed = jnp.pad(framed, ((0, 0), (1, 1), (0, 0), (0, 0)))
    decoded = convolve(framed, conv_weight, conv_bias)
    return (next_latent[None], decoded[None])


def wave_rows():
    pairs_side = HD // 6
    pairs_time = (HD - 4 * pairs_side) // 2
    table = np.zeros((8, HD), np.float32)
    for lane in range(HD):
        pair = lane // 2
        if pair < pairs_time:
            table[0, lane] = np.float32(10000.0 ** (-pair / pairs_time))
        elif pair < pairs_time + pairs_side:
            table[1, lane] = np.float32(10000.0 ** (-(pair - pairs_time) / pairs_side))
        else:
            table[2, lane] = np.float32(10000.0 ** (-(pair - pairs_time - pairs_side) / pairs_side))
            table[3, lane] = 1.0
    return table


MESH = pl.DeviceIdType.MESH
F32 = jnp.float32
BF16 = jnp.bfloat16
NB, NS, NM = 4, 2, 4
TOK, CTXR, WID, NH = 128, 64, 640, 5
KEYS = TOK + CTXR


def dot(a, b):
    return lax.dot_general(a, b, (((1,), (0,)), ((), ())), preferred_element_type=F32)


def dot_nt(a, b):
    return lax.dot_general(a, b, (((1,), (1,)), ((), ())), preferred_element_type=F32)


def dot_tn(a, b):
    return lax.dot_general(a, b, (((0,), (0,)), ((), ())), preferred_element_type=F32)


def step_kernel(
    fo_hbm, noisy_hbm, step_hbm, q_hbm, k_hbm, v_hbm, ck_hbm, cv_hbm, qg_hbm, kg_hbm, gate_hbm,
    hw_hbm, cw_hbm, cb_hbm, waves_hbm,
    next_out, dec_out,
    fo, noisy, step, q_in, k_in, v_in, ck_in, qg, kg, gate, wt, cw, cb, waves, in_sem,
    qall, kbuf, vctx, ckrot, vt, ebuf, numer, st_own, st_prev, dmine, dother, gatet,
    part, rs, nl, lp, nz, sig_now, sig_step, wbig, fr, stage,
    q_send, q_recv, c_send, c_recv, s_send, s_recv, sp_recv, d_send, d_recv,
    r_send, r_recv, n_send, n_recv, l_send, l_recv,
):
    b = lax.axis_index("block")
    s = lax.axis_index("seq")
    m = lax.axis_index("mp")
    nb = lax.rem(b + 1, NB)
    pb = lax.rem(b + NB - 1, NB)
    other = 1 - s

    barrier = pltpu.get_barrier_semaphore()
    for ds in range(NS):
        for dm in range(NM):
            ss, mm = lax.rem(s + ds, NS), lax.rem(m + dm, NM)
            if ds or dm:
                pl.semaphore_signal(barrier, inc=1, device_id=(b, ss, mm), device_id_type=MESH)
            pl.semaphore_signal(barrier, inc=1, device_id=(pb, ss, mm), device_id_type=MESH)

    loads = {}
    for i, (name, src, dst) in enumerate((
        ("fo", fo_hbm, fo), ("waves", waves_hbm, waves), ("q", q_hbm, q_in), ("qg", qg_hbm, qg),
        ("ck", ck_hbm, ck_in), ("kg", kg_hbm, kg), ("k", k_hbm, k_in), ("step", step_hbm, step),
        ("v", v_hbm, v_in), ("cw", cw_hbm, cw), ("gate", gate_hbm, gate), ("wt", hw_hbm, wt),
        ("noisy", noisy_hbm, noisy), ("cb", cb_hbm, cb),
    )):
        loads[name] = pltpu.make_async_copy(src, dst, in_sem.at[i])
        loads[name].start()

    lane = lax.broadcasted_iota(jnp.int32, (8, HD), 1)
    even = lax.rem(lane, 2) == 0
    sign = jnp.where(even, -1.0, 1.0)[0:1]
    row8 = lax.broadcasted_iota(jnp.int32, (8, HD), 0)
    loads["fo"].wait()
    loads["waves"].wait()
    base = fo[b]
    tau = jnp.where(row8 == 2, base + 1, base + s).astype(F32)
    hpos = jnp.where(row8 == 2, s, jnp.where(row8 == 1, 1, 0)).astype(F32)
    ang = tau * waves[0:1] + hpos * waves[1:2]
    cos_r, sin_r = jnp.cos(ang), jnp.sin(ang)
    wpos = lax.broadcasted_iota(jnp.int32, (64, HD), 0).astype(F32)
    ang_c = wpos * waves[2:3]
    cos_c, sin_c = jnp.cos(ang_c), jnp.sin(ang_c)
    col_lane = jnp.broadcast_to(waves[3:4], (64, HD)) > 0.5

    def table(r):
        c = jnp.where(col_lane, cos_c, jnp.broadcast_to(cos_r[r : r + 1], (64, HD)))
        n = jnp.where(col_lane, sin_c, jnp.broadcast_to(sin_r[r : r + 1], (64, HD)))
        return c, n * sign

    c0, n0 = table(0)
    c1, n1 = table(1)
    cos_t = jnp.concatenate([c0, c1], 0)
    sin_t = jnp.concatenate([n0, n1], 0)
    cos_x, sin_x = table(2)

    pr = lax.broadcasted_iota(jnp.int32, (HD, HD), 0)
    pc = lax.broadcasted_iota(jnp.int32, (HD, HD), 1)
    swap = jnp.where(pc == pr + 1 - 2 * lax.rem(pr, 2), 1.0, 0.0).astype(BF16)

    def swapped(g):
        g8 = jnp.broadcast_to(g, (8, HD))
        return jnp.where(even, pltpu.roll(g8, HD - 1, 1), pltpu.roll(g8, 1, 1))[0:1]

    def rotated(x_ref, gain, ct, st, store):
        total = None
        for h in range(NH):
            sl = slice(h * HD, (h + 1) * HD)
            xb = x_ref[0, :, sl]
            x = xb.astype(F32)
            g = gain[h : h + 1]
            xs = dot(xb, swap)
            store(sl, ((x * g) * ct + (xs * swapped(g)) * st).astype(BF16))
            total = x * x if total is None else total + x * x
        return total

    def store_q(sl, val):
        qall[s, :, sl] = val

    def store_k(sl, val):
        kbuf[0:TOK, sl] = val

    def store_c(sl, val):
        ckrot[:, sl] = val

    loads["q"].wait()
    loads["qg"].wait()
    sq_q = rotated(q_in, qg, cos_t, sin_t, store_q)
    loads["ck"].wait()
    loads["kg"].wait()
    sq_c = rotated(ck_in, kg, cos_x, sin_x, store_c)
    loads["k"].wait()
    sq_k = rotated(k_in, kg, cos_t, sin_t, store_k)
    row_q = jnp.sum(sq_q.T, axis=0, keepdims=True)
    row_k = jnp.sum(sq_k.T, axis=0, keepdims=True)
    sq_c2 = jnp.concatenate([sq_c, jnp.zeros((64, HD), F32)], 0)
    row_c = jnp.sum(sq_c2.T, axis=0, keepdims=True)
    loads["step"].wait()
    step_row = step[...].astype(F32)
    st_own[s, m] = jnp.where(
        row8 == 0, row_q, jnp.where(row8 == 1, row_k, jnp.where(row8 == 2, row_c, step_row))
    )

    pl.semaphore_wait(barrier, 2 * NS * NM - 1)

    def remote(src, dst, send, recv, dev):
        return pltpu.make_async_remote_copy(
            src_ref=src, dst_ref=dst, send_sem=send, recv_sem=recv, device_id=dev,
            device_id_type=MESH,
        )

    pend = []

    def go(*args):
        copy = remote(*args)
        copy.start()
        pend.append(copy)

    i = 0
    for ds in range(NS):
        for dm in range(NM):
            ss, mm = lax.rem(s + ds, NS), lax.rem(m + dm, NM)
            if ds or dm:
                go(st_own.at[s, m], st_own.at[s, m], s_send.at[i], s_recv.at[s, m], (b, ss, mm))
                i += 1
    for dm in range(NM):
        mm = lax.rem(m + dm, NM)
        go(st_own.at[s, m], st_prev.at[m], s_send.at[i], sp_recv.at[m], (nb, s, mm))
        i += 1

    for h in range(NH):
        hl = pl.ds(h * HD, HD)
        go(qall.at[s, :, hl], qall.at[s, :, hl], q_send.at[h], q_recv.at[h], (b, other, m))
        go(ckrot.at[:, hl], kbuf.at[pl.ds(TOK, CTXR), hl], c_send.at[h], c_recv.at[h], (nb, s, m))
    go(cv_hbm.at[0], vctx, c_send.at[NH], c_recv.at[NH], (nb, s, m))

    loads["v"].wait()
    for h in range(NH):
        sl = slice(h * HD, (h + 1) * HD)
        vt[sl, 0:TOK] = v_in[0, :, sl].astype(F32).T.astype(BF16)
    steps_col = jnp.broadcast_to(step_row, (HD, HD)).T
    lane64 = lax.broadcasted_iota(jnp.int32, (64, HD), 1)
    steps2 = jnp.where(lane64 < 64, steps_col[0:64], steps_col[64:128])
    loads["noisy"].wait()
    t = jnp.concatenate([noisy[0], jnp.zeros((64, HD), F32)], 0).T
    nz[...] = jnp.concatenate([t[0:64, 0:64], t[64:128, 0:64]], 1)

    def level(at):
        remain = 1.0 - at / STEPS
        return 8.0 * remain / (1.0 + 7.0 * remain)

    now = level(steps2)
    sig_now[...] = now
    sig_step[...] = level(steps2 + 1.0) - now
    lp[:, :, 0:16, :] = jnp.zeros((2, 2, 16, HD), BF16)
    lp[:, :, 80:96, :] = jnp.zeros((2, 2, 16, HD), BF16)
    wbig[...] = jnp.zeros(wbig.shape, BF16)
    loads["cw"].wait()
    for qo in range(2):
        for a in range(3):
            for j in range(2):
                for qi in range(2):
                    d = qo + 2 * j + qi - 1
                    if not 0 <= d <= 2:
                        continue
                    for y in range(4):
                        for yo in range(4):
                            t = y - yo + 1
                            if not 0 <= t <= 2:
                                continue
                            r = a * 256 + j * 128 + y * 32 + qi * 16
                            wbig[qo, r : r + 16, yo * 128 : yo * 128 + 96] = cw[a, t, d]

    for ds in range(NS):
        for dm in range(NM):
            if ds or dm:
                ss, mm = lax.rem(s + ds, NS), lax.rem(m + dm, NM)
                remote(st_own.at[ss, mm], st_own.at[ss, mm], s_send.at[0], s_recv.at[ss, mm],
                       (b, other, m)).wait_recv()
    for mm in range(NM):
        remote(st_prev.at[mm], st_prev.at[mm], s_send.at[0], sp_recv.at[mm],
               (b, other, m)).wait_recv()
    inv = 1.0 / (HEADS * HD)
    qstat = [st_own[e, 0] + st_own[e, 1] + st_own[e, 2] + st_own[e, 3] for e in range(NS)]
    kstat = st_own[s, 0] + st_own[s, 1] + st_own[s, 2] + st_own[s, 3]
    cstat = st_prev[0] + st_prev[1] + st_prev[2] + st_prev[3]
    scale = 1.4426950408889634 / math.sqrt(HD)
    fq = [lax.rsqrt(x[0:1] * inv + 1e-06) * scale for x in qstat]
    fk_own = jnp.broadcast_to(lax.rsqrt(kstat[1:2] * inv + 1e-06), (HD, HD)).T
    fk_ctx = jnp.broadcast_to(lax.rsqrt(cstat[2:3] * inv + 1e-06), (HD, HD)).T[0:CTXR]
    fk = jnp.concatenate([fk_own, fk_ctx], 0)
    factor = jnp.concatenate([fk * fq[0], fk * fq[1]], 1)

    steps_all = jnp.concatenate([st_own[0, 0][3:4], st_own[1, 0][3:4]], 1)
    which = lax.broadcasted_iota(jnp.int32, (STEPS, 2 * TOK), 0).astype(F32)
    hot = jnp.where(which == steps_all, 1.0, 0.0).astype(BF16)
    loads["gate"].wait()
    g_all = gate[...]
    g_hi = g_all.astype(BF16)
    g_lo = (g_all - g_hi.astype(F32)).astype(BF16)
    gatet[...] = dot_tn(g_hi, hot) + dot_tn(g_lo, hot)

    has_prior = jnp.broadcast_to(b, (CTXR, 2 * TOK)) > 0
    sub = lax.broadcasted_iota(jnp.int32, (8, 2 * TOK), 0)
    sums = jnp.ones((8, 2 * TOK), F32)
    for h in range(NH):
        sl = slice(h * HD, (h + 1) * HD)
        hl = pl.ds(h * HD, HD)
        remote(qall.at[s, :, hl], qall.at[other, :, hl], q_send.at[h], q_recv.at[h],
               (b, other, m)).wait_recv()
        remote(ckrot.at[:, hl], kbuf.at[pl.ds(TOK, CTXR), hl], c_send.at[h], c_recv.at[h],
               (b, other, m)).wait_recv()
        qh = jnp.concatenate([qall[0, :, sl], qall[1, :, sl]], 0)
        sc = dot_nt(kbuf[:, sl], qh) * factor
        e = jnp.exp2(sc)
        e_own = e[0:TOK]
        e_ctx = jnp.where(has_prior, e[TOK:KEYS], 0.0)
        den = jnp.sum(e_own, axis=0, keepdims=True) + jnp.sum(e_ctx, axis=0, keepdims=True)
        sums = jnp.where(sub == h, den, sums)
        ebuf[h, 0:TOK] = e_own.astype(BF16)
        ebuf[h, TOK:KEYS] = e_ctx.astype(BF16)
    dmine[...] = sums
    go(dmine, dother, d_send, d_recv, (b, other, m))
    remote(vctx, vctx, c_send.at[NH], c_recv.at[NH], (b, other, m)).wait_recv()
    for h in range(NH):
        sl = slice(h * HD, (h + 1) * HD)
        vt[sl, TOK:KEYS] = vctx[:, sl].astype(F32).T.astype(BF16)
    for h in range(NH):
        sl = slice(h * HD, (h + 1) * HD)
        numer[sl] = dot(vt[sl, :], ebuf[h]) * gatet[sl]
    remote(dmine, dother, d_send, d_recv, (b, other, m)).wait_recv()
    recip = 1.0 / (dmine[...] + dother[...])
    loads["wt"].wait()
    vel_t = jnp.zeros((64, 2 * TOK), F32)
    for h in range(NH):
        sl = slice(h * HD, (h + 1) * HD)
        vel_t += dot(wt[:, sl], (numer[sl] * recip[h : h + 1]).astype(BF16))
    for f in range(2):
        t = jnp.concatenate([vel_t[:, f * TOK : (f + 1) * TOK], jnp.zeros((64, HD), F32)], 0).T
        part[f] = jnp.concatenate([t[0:64, 0:64], t[64:128, 0:64]], 1)

    def cols(mm):
        return pl.ds(pl.multiple_of(mm * 16, 16), 16)

    def lcols(mm):
        return pl.ds(pl.multiple_of(mm * 16 + 16, 16), 16)

    i = 0
    for ds in range(NS):
        for dm in range(NM):
            if ds or dm:
                ss, mm = lax.rem(s + ds, NS), lax.rem(m + dm, NM)
                go(part.at[ss, cols(mm)], rs.at[s, m], r_send.at[i], r_recv.at[s, m], (b, ss, mm))
                i += 1
    rs[s, m] = part[s, cols(m)]
    for ds in range(NS):
        for dm in range(NM):
            if ds or dm:
                ss, mm = lax.rem(s + ds, NS), lax.rem(m + dm, NM)
                remote(rs.at[ss, mm], rs.at[ss, mm], r_send.at[0], r_recv.at[ss, mm],
                       (b, other, m)).wait_recv()
    vel = rs[0, 0]
    for e in range(1, NS * NM):
        vel = vel + rs[e // NM, e % NM]
    latent = nz[cols(m), :]
    lp[1, s, lcols(m), :] = (latent - sig_now[cols(m), :] * vel).astype(BF16)
    mine = lp.at[1, s, lcols(m)]
    i = 0
    for ds in range(NS):
        for dm in range(NM):
            ss, mm = lax.rem(s + ds, NS), lax.rem(m + dm, NM)
            go(mine, lp.at[0, s, lcols(m)], l_send.at[i], l_recv.at[0, s, m], (nb, ss, mm))
            i += 1
            if ds or dm:
                go(mine, mine, l_send.at[i], l_recv.at[1, s, m], (b, ss, mm))
                i += 1
    nl[cols(m), :] = latent + sig_step[cols(m), :] * vel
    for dm in range(1, NM):
        mm = lax.rem(m + dm, NM)
        go(nl.at[cols(m)], nl.at[cols(m)], n_send.at[dm - 1], n_recv.at[m], (b, s, mm))

    for c in (1, 0):
        for ds in range(NS):
            for dm in range(NM):
                if c == 0 or ds or dm:
                    ss, mm = lax.rem(s + ds, NS), lax.rem(m + dm, NM)
                    at = lp.at[c, ss, lcols(mm)]
                    remote(at, at, l_send.at[0], l_recv.at[c, ss, mm], (b, other, m)).wait_recv()
    slab = pl.ds(pl.multiple_of(s * 32, 32), 64)
    prior2 = jnp.broadcast_to(b, (64, HD)) > 0
    for f in range(2):
        fr[f] = jnp.where(prior2, lp[0, f, slab, :].astype(F32), 0.0)
        fr[2 + f] = lp[1, f, slab, :].astype(F32)
    loads["cb"].wait()
    bias = cb[...]
    for qo in range(2):
        rows = []
        for t in range(2):
            taps = []
            for a in range(3):
                for j in range(2):
                    taps.append(fr[t + a, 15 + qo + j : 47 + qo + j, :].astype(BF16))
            rows.append(jnp.concatenate(taps, 1))
        res = dot(jnp.concatenate(rows, 0), wbig[qo])
        for t in range(2):
            for y in range(4):
                stage[t * 4 + y, pl.ds(qo, 32, stride=2), :] = res[
                    t * 32 : (t + 1) * 32, y * 128 : (y + 1) * 128
                ]
    for t in range(2):
        for y in range(4):
            dec_out[0, t, y] = (stage[t * 4 + y][:, 0:96] + bias).astype(BF16)

    for dm in range(1, NM):
        mm = lax.rem(m + dm, NM)
        remote(nl.at[cols(mm)], nl.at[cols(mm)], n_send.at[0], n_recv.at[mm],
               (b, other, m)).wait_recv()
    final = jnp.concatenate([nl[...], jnp.zeros((64, HD), F32)], 0).T
    next_out[0] = jnp.concatenate([final[0:64, 0:64], final[64:128, 0:64]], 1)
    for copy in pend:
        copy.wait_send()


def fused_body(
    noisy_latent, step_index, frame_offset, query_input, key_input, value_input, context_keys,
    context_values, query_gain, key_gain, gate_table, head_weight, conv_weight, conv_bias,
):
    vmem = pl.BlockSpec(memory_space=pltpu.VMEM)
    dma = pltpu.SemaphoreType.DMA
    scratch = [
        pltpu.SMEM((4,), jnp.int32),
        pltpu.VMEM((1, 64, TOK), F32),
        pltpu.VMEM((1, TOK), jnp.int32),
        pltpu.VMEM((1, TOK, WID), BF16),
        pltpu.VMEM((1, TOK, WID), BF16),
        pltpu.VMEM((1, TOK, WID), BF16),
        pltpu.VMEM((1, CTXR, WID), BF16),
        pltpu.VMEM((NH, HD), F32),
        pltpu.VMEM((NH, HD), F32),
        pltpu.VMEM((STEPS, WID), F32),
        pltpu.VMEM((64, WID), BF16),
        pltpu.VMEM((3, 3, 3, LAT, 96), BF16),
        pltpu.VMEM((1, 96), F32),
        pltpu.VMEM((8, HD), F32),
        dma((14,)),
        pltpu.VMEM((2, TOK, WID), BF16),
        pltpu.VMEM((KEYS, WID), BF16),
        pltpu.VMEM((CTXR, WID), BF16),
        pltpu.VMEM((CTXR, WID), BF16),
        pltpu.VMEM((WID, KEYS), BF16),
        pltpu.VMEM((NH, KEYS, 2 * TOK), BF16),
        pltpu.VMEM((WID, 2 * TOK), F32),
        pltpu.VMEM((NS, NM, 8, HD), F32),
        pltpu.VMEM((NM, 8, HD), F32),
        pltpu.VMEM((8, 2 * TOK), F32),
        pltpu.VMEM((8, 2 * TOK), F32),
        pltpu.VMEM((WID, 2 * TOK), F32),
        pltpu.VMEM((2, 64, HD), F32),
        pltpu.VMEM((NS, NM, 16, HD), F32),
        pltpu.VMEM((64, HD), F32),
        pltpu.VMEM((2, 2, 96, HD), BF16),
        pltpu.VMEM((64, HD), F32),
        pltpu.VMEM((64, HD), F32),
        pltpu.VMEM((64, HD), F32),
        pltpu.VMEM((2, 768, 512), BF16),
        pltpu.VMEM((4, 64, HD), F32),
        pltpu.VMEM((8, 64, HD), F32),
        dma((NH,)), dma((NH,)), dma((NH + 1,)), dma((NH + 1,)),
        dma((11,)), dma((NS, NM)), dma((NM,)),
        dma, dma,
        dma((7,)), dma((NS, NM)),
        dma((3,)), dma((NM,)),
        dma((15,)), dma((2, NS, NM)),
    ]
    hbm = pl.BlockSpec(memory_space=pltpu.HBM)
    next_latent, decoded = pl.pallas_call(
        step_kernel,
        out_shape=(
            jax.ShapeDtypeStruct((1, 64, TOK), F32),
            jax.ShapeDtypeStruct((1, 2, 4, 64, 96), BF16),
        ),
        in_specs=[hbm] * 15,
        out_specs=(vmem, vmem),
        scratch_shapes=scratch,
        compiler_params=pltpu.CompilerParams(
            collective_id=0, has_side_effects=True, vmem_limit_bytes=32 * 1024 * 1024
        ),
    )(*[pltpu.with_memory_space_constraint(x, pltpu.HBM) for x in (
        frame_offset, noisy_latent.transpose(0, 2, 1), step_index, query_input, key_input, value_input,
        context_keys, context_values, query_gain.reshape(NH, HD), key_gain.reshape(NH, HD),
        gate_table, head_weight.T, conv_weight, conv_bias.reshape(1, -1),
        jnp.asarray(wave_rows()),
    )])
    return next_latent.transpose(0, 2, 1), decoded


def fused_fits(mesh):
    return dict(mesh.shape) == {"block": NB, "seq": NS, "mp": NM}


def solution(mesh):
    return jax.shard_map(
        fused_body if fused_fits(mesh) else body,
        mesh=mesh,
        in_specs=(
            P("block", "seq", None),
            P("block", "seq"),
            P(),
            P("block", "seq", "mp"),
            P("block", "seq", "mp"),
            P("block", "seq", "mp"),
            P("block", "seq", "mp"),
            P("block", "seq", "mp"),
            P("mp"),
            P("mp"),
            P(None, "mp"),
            P("mp", None),
            P(None, None, None, None, "mp"),
            P("mp"),
        ),
        out_specs=(P("block", "seq", None), P("block", None, None, "seq", "mp")),
        check_vma=False,
    )
```
